256 devices in a mesh: ctx: 64 (over y_hi, z, x), tp: 4 (over y_lo, core).
Axes of the slice: x: 4, y: 4 (y_hi: 2, y_lo: 2; y = y_hi * 2 + y_lo), z: 8, core: 2. Of those that a mesh axis runs over, the one named last changes fastest.
Arguments:
- queries: bfloat16 [8192, 2048], P('ctx', 'tp'), may hold values from -6 to 6
- key_rows: bfloat16 [8192, 512], P('ctx', 'tp'), may hold values from -6 to 6
- value_matrix: bfloat16 [8192, 512], P('ctx', 'tp'), may hold values from -6 to 6
- attention_out: bfloat16 [8192, 2048], P('ctx', 'tp'), may hold values from -6 to 6
- output_grad: bfloat16 [8192, 2048], P('ctx', 'tp'), may hold values from -6 to 6
- w_query: bfloat16 [2048, 2048], P(None, 'tp'), may hold values from -3 to 3
- key_weight: bfloat16 [2048, 512], P(None, 'tp'), may hold values from -3 to 3
- value_weight: bfloat16 [2048, 512], P(None, 'tp'), may hold values from -3 to 3
- span_pos: int32 [128], replicated, may hold values from 0 to 127, as said below
Outputs:
- input_grad: bfloat16 [8192, 2048], P('ctx', 'tp')
The draws below stay inside these ranges and needn't reach their ends.
Inputs may be any that keep to these rules, and one draw needn't show every extreme that they name: Device d of ctx stores spans 2d and 2d + 1; their positions span_pos[2d] and span_pos[2d + 1] add up to 127, in either order; every position appears once.
All inputs are finite; a program needn't handle non-finite values.
Results may differ from the reference program's by a relative error of at most 0.0056.
Values may be sent and summed in bfloat16 or wider, within the bound.
No kernel may reach another device: no remote copies, remote signals or barrier semaphores. Data moves between devices by JAX's collectives and lax.ppermute only.
A program may use at most 64 MiB of HBM per device.

```python
import jax
import jax.numpy as jnp
from jax import lax

MODEL_WIDTH = 2048
QUERY_HEADS = 16
KEY_VALUE_HEADS = 4
HEAD_SIZE = 128
SPAN_TOKENS = 64
SPAN_COUNT = 128
TOKEN_COUNT = 8192


def draw_queries(key, part):
    key = jax.random.fold_in(key, 11)
    base_offset = jnp.clip(jax.random.normal(key, (SPAN_COUNT, SPAN_TOKENS, QUERY_HEADS, HEAD_SIZE), jnp.float32), -6.0, 6.0)
    return base_offset.reshape(TOKEN_COUNT, QUERY_HEADS * HEAD_SIZE).astype(jnp.bfloat16)


def draw_key_rows(key, part):
    key = jax.random.fold_in(key, 23)
    base_offset = jnp.clip(jax.random.normal(key, (SPAN_COUNT, SPAN_TOKENS, KEY_VALUE_HEADS, HEAD_SIZE), jnp.float32), -6.0, 6.0)
    return base_offset.reshape(TOKEN_COUNT, KEY_VALUE_HEADS * HEAD_SIZE).astype(jnp.bfloat16)


def draw_span_pos(key, part):
    key = jax.random.fold_in(key, 37)
    order_key, flip_key = jax.random.split(key)
    lower = jax.random.permutation(order_key, SPAN_COUNT // 2).astype(jnp.int32)
    upper = (SPAN_COUNT - 1 - lower).astype(jnp.int32)
    flips = jax.random.randint(flip_key, (SPAN_COUNT // 2,), 0, 2, jnp.int32)
    first = jnp.where(flips == 0, lower, upper)
    second = jnp.where(flips == 0, upper, lower)
    return jnp.stack((first, second), axis=1).reshape(SPAN_COUNT).astype(jnp.int32)


def level_of(rng, dims, cuts, low, high):
    loudness = 1.0
    for axis_at, shards_of in cuts:
        steps = jax.random.uniform(jax.random.fold_in(jax.random.fold_in(rng, 6), axis_at), (shards_of,), jnp.float32, low / len(cuts), high / len(cuts))
        loudness = loudness * jnp.repeat(jnp.exp(steps), dims[axis_at] // shards_of).reshape((-1,) + (1,) * (len(dims) - 1 - axis_at))
    return loudness


def centred(rng, extent, spread, bound, pieces=(), kind=jnp.bfloat16):
    result = jax.random.normal(rng, extent, jnp.float32) * spread
    if len(pieces) > 0:
        result = level_of(rng, extent, pieces, -0.22, 0.18) * result
    return jnp.clip(result, min=-bound, max=bound).astype(kind)


def setup_inputs(seed: int = 0) -> dict:
    keys = jax.random.split(jax.random.key(seed), 10)
    return {
        "queries": draw_queries(jax.random.fold_in(keys[9], 71), 0),
        "key_rows": draw_key_rows(jax.random.fold_in(keys[9], 71), 0),
        "value_matrix": centred(keys[2], (TOKEN_COUNT, KEY_VALUE_HEADS * HEAD_SIZE), 1.0, 6.0, ((0, 64), (1, 4))),
        "attention_out": centred(keys[3], (TOKEN_COUNT, QUERY_HEADS * HEAD_SIZE), 1.0, 6.0, ((0, 64), (1, 4))),
        "output_grad": centred(keys[4], (TOKEN_COUNT, QUERY_HEADS * HEAD_SIZE), 1.0, 6.0, ((0, 64), (1, 4))),
        "w_query": centred(keys[5], (MODEL_WIDTH, QUERY_HEADS * HEAD_SIZE), 0.5, 3.0, ((1, 4),)),
        "key_weight": centred(keys[6], (MODEL_WIDTH, KEY_VALUE_HEADS * HEAD_SIZE), 0.5, 3.0, ((1, 4),)),
        "value_weight": centred(keys[7], (MODEL_WIDTH, KEY_VALUE_HEADS * HEAD_SIZE), 0.5, 3.0, ((1, 4),)),
        "span_pos": draw_span_pos(jax.random.fold_in(keys[9], 71), 0),
    }


def head_backward(query, grad_rows, deltas, key_rows, value_matrix):
    group_width = QUERY_HEADS // KEY_VALUE_HEADS
    score_scale = HEAD_SIZE ** -0.5
    key_block = min(512, TOKEN_COUNT)
    rows_block = key_block * group_width
    block_total = TOKEN_COUNT // key_block
    key_offsets = jnp.arange(key_block, dtype=jnp.int32)
    row_pos = jnp.repeat(jnp.arange(TOKEN_COUNT, dtype=jnp.int32), group_width)

    def scores_of(block_row, block_col):
        q_block = lax.dynamic_slice_in_dim(query, block_row * rows_block, rows_block, 0)
        k_block = lax.dynamic_slice_in_dim(key_rows, block_col * key_block, key_block, 0)
        raw_scores = jnp.dot(q_block, k_block.T, preferred_element_type=jnp.float32) * score_scale
        q_pos = lax.dynamic_slice_in_dim(row_pos, block_row * rows_block, rows_block, 0)
        allowed = (block_col * key_block + key_offsets)[None, :] <= q_pos[:, None]
        return raw_scores, allowed

    def row_stats(block_row):
        def stats_step(block_col, running):
            run_max, run_sum = running
            block_col = block_col.astype(jnp.int32)
            raw_scores, allowed = scores_of(block_row, block_col)
            masked = jnp.where(allowed, raw_scores, -jnp.inf)
            new_max = jnp.maximum(run_max, jnp.max(masked, axis=1))
            run_sum = run_sum * jnp.exp(run_max - new_max) + jnp.sum(jnp.exp(masked - new_max[:, None]), axis=1)
            return new_max, run_sum

        start_stats = (jnp.full((rows_block,), -jnp.inf, jnp.float32), jnp.zeros((rows_block,), jnp.float32))
        run_max, run_sum = lax.fori_loop(0, block_row + 1, stats_step, start_stats)
        return run_max + jnp.log(run_sum)

    log_totals = lax.map(row_stats, jnp.arange(block_total, dtype=jnp.int32)).reshape(-1)

    def query_block(outer, block_row):
        q_block = lax.dynamic_slice_in_dim(query, block_row * rows_block, rows_block, 0)
        g_block = lax.dynamic_slice_in_dim(grad_rows, block_row * rows_block, rows_block, 0)
        lse_block = lax.dynamic_slice_in_dim(log_totals, block_row * rows_block, rows_block, 0)
        delta_block = lax.dynamic_slice_in_dim(deltas, block_row * rows_block, rows_block, 0)

        def grad_step(block_col, inner):
            query_acc, key_acc, value_acc = inner
            block_col = block_col.astype(jnp.int32)
            raw_scores, allowed = scores_of(block_row, block_col)
            weights = jnp.where(allowed, jnp.exp(raw_scores - lse_block[:, None]), 0.0)
            probs_low = weights.astype(jnp.bfloat16)
            k_block = lax.dynamic_slice_in_dim(key_rows, block_col * key_block, key_block, 0)
            v_block = lax.dynamic_slice_in_dim(value_matrix, block_col * key_block, key_block, 0)
            grad_probs = jnp.dot(g_block, v_block.T, preferred_element_type=jnp.float32)
            grad_scores = (weights * (grad_probs - delta_block[:, None])).astype(jnp.bfloat16)
            query_acc = query_acc + jnp.dot(grad_scores, k_block, preferred_element_type=jnp.float32) * score_scale
            part_key = jnp.dot(grad_scores.T, q_block, preferred_element_type=jnp.float32) * score_scale
            part_value = jnp.dot(probs_low.T, g_block, preferred_element_type=jnp.float32)
            first_row = block_col * key_block
            key_acc = lax.dynamic_update_slice_in_dim(key_acc, lax.dynamic_slice_in_dim(key_acc, first_row, key_block, 0) + part_key, first_row, 0)
            value_acc = lax.dynamic_update_slice_in_dim(value_acc, lax.dynamic_slice_in_dim(value_acc, first_row, key_block, 0) + part_value, first_row, 0)
            return query_acc, key_acc, value_acc

        start_rows = jnp.zeros((rows_block, HEAD_SIZE), jnp.float32)
        query_acc, key_acc, value_acc = lax.fori_loop(0, block_row + 1, grad_step, (start_rows, outer[0], outer[1]))
        return (key_acc, value_acc), query_acc

    zero_keys = jnp.zeros((TOKEN_COUNT, HEAD_SIZE), jnp.float32)
    (key_acc, value_acc), query_acc = lax.scan(query_block, (zero_keys, zero_keys), jnp.arange(block_total, dtype=jnp.int32))
    return query_acc.reshape(TOKEN_COUNT, group_width * HEAD_SIZE), key_acc, value_acc


def reference(queries, key_rows, value_matrix, attention_out, output_grad, w_query, key_weight, value_weight, span_pos):
    group_width = QUERY_HEADS // KEY_VALUE_HEADS
    row_ids = jnp.arange(TOKEN_COUNT, dtype=jnp.int32)
    position = (span_pos[row_ids // SPAN_TOKENS] * SPAN_TOKENS + row_ids % SPAN_TOKENS).astype(jnp.int32)
    inverse = jnp.zeros((TOKEN_COUNT,), jnp.int32).at[position].set(row_ids)
    query_sorted = queries[inverse].reshape(TOKEN_COUNT, QUERY_HEADS, HEAD_SIZE)
    grad_sorted = output_grad[inverse].reshape(TOKEN_COUNT, QUERY_HEADS, HEAD_SIZE)
    key_sorted = key_rows[inverse]
    value_sorted = value_matrix[inverse]
    products = output_grad.astype(jnp.float32) * attention_out.astype(jnp.float32)
    delta_sorted = jnp.sum(products.reshape(TOKEN_COUNT, QUERY_HEADS, HEAD_SIZE), axis=2)[inverse]
    query_parts, key_parts, value_parts = [], [], []
    for head_number in range(KEY_VALUE_HEADS):
        low = head_number * group_width
        high = low + group_width
        query_head = query_sorted[:, low:high].reshape(TOKEN_COUNT * group_width, HEAD_SIZE)
        grad_head = grad_sorted[:, low:high].reshape(TOKEN_COUNT * group_width, HEAD_SIZE)
        delta_head = delta_sorted[:, low:high].reshape(TOKEN_COUNT * group_width)
        part_query, part_key, part_value = head_backward(query_head, grad_head, delta_head, key_sorted[:, head_number * HEAD_SIZE:(head_number + 1) * HEAD_SIZE], value_sorted[:, head_number * HEAD_SIZE:(head_number + 1) * HEAD_SIZE])
        query_parts.append(part_query)
        key_parts.append(part_key)
        value_parts.append(part_value)
    grad_query = jnp.concatenate(query_parts, axis=1)[position].astype(jnp.bfloat16)
    grad_key = jnp.concatenate(key_parts, axis=1)[position].astype(jnp.bfloat16)
    grad_value = jnp.concatenate(value_parts, axis=1)[position].astype(jnp.bfloat16)
    total = jnp.dot(grad_query, w_query.T, preferred_element_type=jnp.float32)
    total = total + jnp.dot(grad_key, key_weight.T, preferred_element_type=jnp.float32)
    total = total + jnp.dot(grad_value, value_weight.T, preferred_element_type=jnp.float32)
    return total.astype(jnp.bfloat16)
```

```python
import functools
import math

import jax
import jax.numpy as jnp
from jax import lax
from jax.experimental import pallas as pl
from jax.experimental.pallas import tpu as pltpu
from jax.sharding import PartitionSpec as P

HEAD = 128
SPAN = 64
GROUP = 4
QUERY_SHARE = 4
SUBS = 4
BLOCK = SUBS * SPAN
COLS = GROUP * SPAN
SCALE = HEAD ** (-0.5)
SCALE2 = SCALE * math.log2(math.e)
LOG2E = math.log2(math.e)
NEG = -1e30
F32 = jnp.float32
BF16 = jnp.bfloat16


def dot(left, right, left_dim, right_dim):
    return lax.dot_general(
        left, right, (((left_dim,), (right_dim,)), ((), ())), preferred_element_type=F32
    )


def pack_kernel(q_ref, g_ref, o_ref, out_ref):
    width = GROUP * HEAD
    out_ref[:, :width] = q_ref[...]
    out_ref[:, width : 2 * width] = g_ref[...]
    lane = lax.broadcasted_iota(jnp.int32, (q_ref.shape[0], HEAD), 1)
    extra = jnp.zeros((q_ref.shape[0], HEAD), F32)
    for head in range(GROUP):
        cols = slice(head * HEAD, (head + 1) * HEAD)
        products = g_ref[:, cols].astype(F32) * o_ref[:, cols].astype(F32)
        rest = jnp.sum(products, axis=1, keepdims=True)
        for term in range(3):
            part = rest.astype(BF16).astype(F32)
            extra = jnp.where(lane == term * GROUP + head, part, extra)
            rest = rest - part
    out_ref[:, 2 * width :] = extra.astype(BF16)


def key_row(slot):
    return pl.multiple_of((slot // 2) * (4 * SPAN) + (slot % 2) * SPAN, SPAN)


def stacked(ref, half, first_col):
    rows = slice(half * SPAN, (half + 1) * SPAN)
    return jnp.concatenate(
        [ref[rows, first_col + h * HEAD : first_col + (h + 1) * HEAD] for h in range(GROUP)],
        axis=0,
    )


def mask_pattern():
    row = lax.broadcasted_iota(jnp.int32, (SPAN, COLS), 0)
    col = lax.broadcasted_iota(jnp.int32, (SPAN, COLS), 1)
    return row - col % SPAN


def stats_kernel(spans, meta, kv_ref, p0, p1, p2, p3, out_ref, ks):
    def copy_span(n, carry):
        src = key_row(meta[n])
        ks[pl.ds(pl.multiple_of(n * SPAN, SPAN), SPAN), :] = kv_ref[pl.ds(src, SPAN), :]
        return carry

    lax.fori_loop(0, spans, copy_span, 0)
    pattern = mask_pattern()
    packed = (p0, p1, p2, p3)
    for i in range(2 * QUERY_SHARE):
        query = stacked(packed[i // 2], i % 2, 0)
        query_pos = meta[2 * spans + i]

        def step(block, carry):
            run_max, run_sum = carry
            keys = ks[pl.ds(pl.multiple_of(block * BLOCK, BLOCK), BLOCK), :]
            scores = dot(keys, query, 1, 1) * SCALE2
            parts = []
            new_max = run_max
            for sub in range(SUBS):
                gap = (query_pos - meta[spans + block * SUBS + sub]) * SPAN
                part = jnp.where(pattern <= gap, scores[sub * SPAN : (sub + 1) * SPAN], NEG)
                part = part.reshape(SPAN // 8, 8, COLS)
                new_max = jnp.maximum(new_max, jnp.max(part, axis=0))
                parts.append(part)
            run_sum = run_sum * jnp.exp2(run_max - new_max)
            for part in parts:
                run_sum = run_sum + jnp.sum(jnp.exp2(part - new_max[None]), axis=0)
            return new_max, run_sum

        start = (jnp.full((8, COLS), NEG, F32), jnp.zeros((8, COLS), F32))
        run_max, run_sum = lax.fori_loop(0, meta[2 * spans + 2 * QUERY_SHARE + i], step, start)
        top = jnp.max(run_max, axis=0, keepdims=True)
        out_ref[i : i + 1, :] = top
        total = jnp.sum(run_sum * jnp.exp2(run_max - top), axis=0, keepdims=True)
        out_ref[2 * QUERY_SHARE + i : 2 * QUERY_SHARE + i + 1, :] = total


def grads_kernel(
    spans, meta, kv_ref, p0, p1, p2, p3, s0, s1, s2, s3, dkv_ref, dq0, dq1, dq2, dq3, ks, vs, dka, dva
):
    width = GROUP * HEAD
    minus = jnp.full((SPAN, HEAD), -1.0, BF16)

    def copy_span(n, carry):
        src = key_row(meta[n])
        rows = pl.ds(pl.multiple_of(n * SPAN, SPAN), SPAN)
        ks[rows, :] = kv_ref[pl.ds(src, SPAN), :]
        vs[rows, :HEAD] = kv_ref[pl.ds(pl.multiple_of(src + 2 * SPAN, SPAN), SPAN), :]
        vs[rows, HEAD:] = minus
        return carry

    lax.fori_loop(0, spans, copy_span, 0)
    dka[...] = jnp.zeros_like(dka)
    dva[...] = jnp.zeros_like(dva)
    pattern = mask_pattern()
    lane = lax.broadcasted_iota(jnp.int32, (SPAN, HEAD), 1)
    packed = (p0, p1, p2, p3)
    stats = (s0, s1, s2, s3)
    outs = (dq0, dq1, dq2, dq3)
    for i in range(2 * QUERY_SHARE):
        slot, half = i // 2, i % 2
        query = stacked(packed[slot], half, 0)
        grad = stacked(packed[slot], half, width)
        extra = packed[slot][half * SPAN : (half + 1) * SPAN, 2 * width :].astype(F32)
        extras = jnp.concatenate(
            [
                jnp.where(jnp.logical_and(lane % GROUP == h, lane < 3 * GROUP), extra, 0.0)
                for h in range(GROUP)
            ],
            axis=0,
        ).astype(BF16)
        grad_ext = jnp.concatenate([grad, extras], axis=1)
        query_pos = meta[2 * spans + i]
        tops, sums = [], []
        for shift in range(QUERY_SHARE):
            row = ((slot - shift) % QUERY_SHARE) * 2 + half
            tops.append(stats[shift][row : row + 1, :])
            sums.append(stats[shift][2 * QUERY_SHARE + row : 2 * QUERY_SHARE + row + 1, :])
        top = functools.reduce(jnp.maximum, tops)
        total = sum(s * jnp.exp2(t - top) for s, t in zip(sums, tops))
        log_total = top + jnp.log(total) * LOG2E

        def step(block, query_acc):
            rows = pl.ds(pl.multiple_of(block * BLOCK, BLOCK), BLOCK)
            keys = ks[rows, :]
            scores = dot(keys, query, 1, 1) * SCALE2 - log_total
            weights = []
            for sub in range(SUBS):
                gap = (query_pos - meta[spans + block * SUBS + sub]) * SPAN
                part = jnp.exp2(scores[sub * SPAN : (sub + 1) * SPAN])
                weights.append(jnp.where(pattern <= gap, part, 0.0))
            weights = jnp.concatenate(weights, axis=0)
            grad_probs = dot(vs[rows, :], grad_ext, 1, 1)
            grad_scores = (weights * grad_probs).astype(BF16)
            dva[rows, :] += dot(weights.astype(BF16), grad, 1, 0)
            dka[rows, :] += dot(grad_scores, query, 1, 0)
            return query_acc + dot(grad_scores, keys, 0, 0)

        query_acc = lax.fori_loop(
            0, meta[2 * spans + 2 * QUERY_SHARE + i], step, jnp.zeros((COLS, HEAD), F32)
        )
        for h in range(GROUP):
            outs[slot][half * SPAN : (half + 1) * SPAN, h * HEAD : (h + 1) * HEAD] = (
                query_acc[h * SPAN : (h + 1) * SPAN] * SCALE
            ).astype(outs[slot].dtype)

    def place_span(n, carry):
        dst = key_row(meta[n])
        rows = pl.ds(pl.multiple_of(n * SPAN, SPAN), SPAN)
        dkv_ref[pl.ds(dst, SPAN), :] = (dka[rows, :] * SCALE).astype(BF16)
        dkv_ref[pl.ds(pl.multiple_of(dst + 2 * SPAN, SPAN), SPAN), :] = dva[rows, :].astype(BF16)
        return carry

    lax.fori_loop(0, spans, place_span, 0)


VMEM = pl.BlockSpec(memory_space=pltpu.VMEM)
SMEM = pl.BlockSpec(memory_space=pltpu.SMEM)
PARAMS = pltpu.CompilerParams(vmem_limit_bytes=40 * 1024 * 1024)


def local(q, k, v, o, g, w_query, key_weight, value_weight, span_pos):
    tokens, width = q.shape
    cycle = lax.axis_size("ctx")
    tp_size = lax.axis_size("tp")
    members = cycle // QUERY_SHARE
    spans = 2 * members
    index = lax.axis_index("ctx")
    mine, base = index % QUERY_SHARE, index // QUERY_SHARE * QUERY_SHARE
    key_groups = [[j * QUERY_SHARE + i for j in range(members)] for i in range(QUERY_SHARE)]

    def shifted(array, shift):
        pairs = []
        for device in range(cycle):
            low = device // QUERY_SHARE * QUERY_SHARE
            pairs.append((device, low + (device - low + shift) % QUERY_SHARE))
        return lax.ppermute(array, "ctx", pairs)

    packed = pl.pallas_call(
        pack_kernel,
        out_shape=jax.ShapeDtypeStruct((tokens, 2 * width + HEAD), BF16),
        in_specs=[VMEM] * 3,
        out_specs=VMEM,
        name="pack",
    )(q, g, o)
    packs = [packed] + [shifted(packed, s) for s in range(1, QUERY_SHARE)]
    own_kv = jnp.concatenate([k, v], axis=0)
    copies = jnp.broadcast_to(own_kv[None], (members,) + own_kv.shape).reshape(-1, HEAD)
    kv = lax.all_to_all(copies, "ctx", 0, 0, tiled=True, axis_index_groups=key_groups)

    key_pos = lax.dynamic_slice_in_dim(
        span_pos.reshape(members, QUERY_SHARE, 2), mine, 1, axis=1
    ).reshape(spans)
    ids = jnp.arange(spans, dtype=jnp.int32)
    rank = jnp.sum((key_pos[None, :] < key_pos[:, None]).astype(jnp.int32), axis=1)
    placed = rank[None, :] == ids[:, None]
    order = jnp.sum(jnp.where(placed, ids[None, :], 0), axis=1)
    sorted_pos = jnp.sum(jnp.where(placed, key_pos[None, :], 0), axis=1)
    share_pos = lax.dynamic_slice_in_dim(span_pos, 2 * base, 2 * QUERY_SHARE).reshape(-1, 2)
    turned = (mine - jnp.arange(QUERY_SHARE, dtype=jnp.int32)) % QUERY_SHARE
    query_pos = jnp.sum(
        jnp.where(
            turned[:, None, None] == jnp.arange(QUERY_SHARE, dtype=jnp.int32)[None, :, None],
            share_pos[None],
            0,
        ),
        axis=1,
    ).reshape(-1)
    seen = jnp.sum((key_pos[None, :] <= query_pos[:, None]).astype(jnp.int32), axis=1)
    meta = jnp.concatenate([order, sorted_pos, query_pos, (seen + SUBS - 1) // SUBS])

    stat_rows = 4 * QUERY_SHARE
    stats = pl.pallas_call(
        functools.partial(stats_kernel, spans),
        out_shape=jax.ShapeDtypeStruct((stat_rows, COLS), F32),
        in_specs=[SMEM] + [VMEM] * 5,
        out_specs=VMEM,
        scratch_shapes=[pltpu.VMEM((spans * SPAN, HEAD), BF16)],
        compiler_params=PARAMS,
        name="stats",
    )(meta, kv, *packs)
    all_stats = [stats] + [shifted(stats, s) for s in range(1, QUERY_SHARE)]
    dq_shape = (tokens, width)
    dkv, *dqs = pl.pallas_call(
        functools.partial(grads_kernel, spans),
        out_shape=[jax.ShapeDtypeStruct((2 * spans * SPAN, HEAD), BF16)]
        + [jax.ShapeDtypeStruct(dq_shape, F32)]
        + [jax.ShapeDtypeStruct(dq_shape, BF16)] * (QUERY_SHARE - 1),
        in_specs=[SMEM] + [VMEM] * 9,
        out_specs=[VMEM] * 5,
        scratch_shapes=[
            pltpu.VMEM((spans * SPAN, HEAD), BF16),
            pltpu.VMEM((spans * SPAN, 2 * HEAD), BF16),
            pltpu.VMEM((spans * SPAN, HEAD), F32),
            pltpu.VMEM((spans * SPAN, HEAD), F32),
        ],
        compiler_params=PARAMS,
        name="grads",
    )(meta, kv, *packs, *all_stats)
    dq_parts = [shifted(dqs[s], -s) for s in range(1, QUERY_SHARE)]
    dkv_parts = lax.all_to_all(dkv, "ctx", 0, 0, tiled=True, axis_index_groups=key_groups)
    dq_sum = dqs[0]
    for part in dq_parts:
        dq_sum = dq_sum + part.astype(F32)
    grad_query = dq_sum.astype(BF16)
    dkv_sum = jnp.sum(dkv_parts.reshape(members, 2, tokens, HEAD).astype(F32), axis=0).astype(BF16)
    partial = (
        dot(grad_query, w_query, 1, 1)
        + dot(dkv_sum[0], key_weight, 1, 1)
        + dot(dkv_sum[1], value_weight, 1, 1)
    )
    feats = partial.shape[1] // tp_size
    rank_tp = lax.axis_index("tp")
    total = lax.dynamic_slice_in_dim(partial, rank_tp * feats, feats, 1)
    for s in range(1, tp_size):
        peer = (rank_tp + s) % tp_size
        piece = lax.dynamic_slice_in_dim(partial, peer * feats, feats, 1).astype(BF16)
        pairs = [(d, (d + s) % tp_size) for d in range(tp_size)]
        total = total + lax.ppermute(piece, "tp", pairs).astype(F32)
    return total.astype(BF16)


def solution(mesh):
    row, col = P("ctx", "tp"), P(None, "tp")
    in_specs = (row, row, row, row, row, col, col, col, P())
    return jax.shard_map(local, mesh=mesh, in_specs=in_specs, out_specs=row, check_vma=False)
```

```python
import functools
import math

import jax
import jax.numpy as jnp
from jax import lax
from jax.experimental import pallas as pl
from jax.experimental.pallas import tpu as pltpu
from jax.sharding import PartitionSpec as P

HEAD = 128
SPAN = 64
GROUP = 4
SHARE = 4
SIDES = 2
SUBS = 4
BLOCK = SUBS * SPAN
COLS = GROUP * SPAN
WIDTH = GROUP * HEAD
QSPANS = 2 * SHARE
TURN = 10
SCALE = HEAD ** (-0.5)
LOG2E = math.log2(math.e)
SCALE2 = SCALE * LOG2E
NEG = -1e30
F32 = jnp.float32
BF16 = jnp.bfloat16


def dot(left, right, left_dim, right_dim):
    return lax.dot_general(
        left, right, (((left_dim,), (right_dim,)), ((), ())), preferred_element_type=F32
    )


def rows_at(index, size):
    return pl.ds(pl.multiple_of(index * size, size), size)


def span_rows(slot, value):
    return rows_at(slot // 2 * 4 + slot % 2 + 2 * value, SPAN)


def load_all(sources, buffers, sems):
    copies = [
        pltpu.make_async_copy(source, buffer, sems.at[n])
        for n, (source, buffer) in enumerate(zip(sources, buffers))
    ]
    for copy in copies:
        copy.start()
    return copies


def head_cols(head, first=0):
    return slice(first + head * HEAD, first + (head + 1) * HEAD)


def span_slice(half):
    return slice(half * SPAN, (half + 1) * SPAN)


def part_slice(index, size):
    return slice(index * size, (index + 1) * size)


def tile_kernel(k_ref, v_ref, out_ref):
    tokens = k_ref.shape[0]
    for member in range(out_ref.shape[0] // (2 * tokens)):
        out_ref[part_slice(2 * member, tokens), :] = k_ref[...]
        out_ref[part_slice(2 * member + 1, tokens), :] = v_ref[...]


def pack_kernel(g_ref, o_ref, out_ref):
    out_ref[:, :WIDTH] = g_ref[...]
    lane = lax.broadcasted_iota(jnp.int32, (g_ref.shape[0], HEAD), 1)
    extra = jnp.zeros((g_ref.shape[0], HEAD), F32)
    for head in range(GROUP):
        cols = head_cols(head)
        products = g_ref[:, cols].astype(F32) * o_ref[:, cols].astype(F32)
        rest = jnp.sum(products, axis=1, keepdims=True)
        for term in range(3):
            part = rest.astype(BF16).astype(F32)
            extra = jnp.where(lane == term * GROUP + head, part, extra)
            rest = rest - part
    out_ref[:, WIDTH:] = extra.astype(BF16)


def mask_pattern():
    row = lax.broadcasted_iota(jnp.int32, (SPAN, COLS), 0)
    col = lax.broadcasted_iota(jnp.int32, (SPAN, COLS), 1)
    return row - col % SPAN


def step_of(meta, spans, step):
    at = 2 * spans + 3 * step
    return meta[at], meta[at + 1], meta[at + 2]


def stats_kernel(
    spans, steps, meta, kv_ref, q0, q1, q2, q3, before, out_ref, kin, qin, ks, qs, ms, ls, sems
):
    copies = load_all((kv_ref, q0, q1, q2, q3), (kin, *[qin.at[n] for n in range(SHARE)]), sems)
    copies[0].wait()

    def copy_span(n, carry):
        ks[rows_at(n, SPAN), :] = kin[span_rows(meta[n], 0), :]
        return carry

    lax.fori_loop(0, spans, copy_span, 0, unroll=8)
    for copy in copies[1:]:
        copy.wait()
    for i in range(QSPANS):
        for h in range(GROUP):
            qs[part_slice(i * GROUP + h, SPAN), :] = qin[i // 2, span_slice(i % 2), head_cols(h)]
    ms[...] = jnp.full_like(ms, NEG)
    ls[...] = jnp.zeros_like(ls)
    pattern = mask_pattern()

    def turn(index, carry):
        todo = [step_of(meta, spans, index * TURN + u) for u in range(TURN)]
        scores = [
            dot(ks[rows_at(block, BLOCK), :], qs[rows_at(q_at, COLS), :], 1, 1)
            for q_at, block, _ in todo
        ]
        tops, totals = [], []
        for (_, block, query_pos), score in zip(todo, scores):
            parts = []
            for sub in range(SUBS):
                gap = (query_pos - meta[spans + block * SUBS + sub]) * SPAN
                part = jnp.where(pattern <= gap, score[part_slice(sub, SPAN)] * SCALE2, NEG)
                parts.append(part.reshape(SPAN // 8, 8, COLS))
            top = functools.reduce(jnp.maximum, [jnp.max(part, axis=0) for part in parts])
            tops.append(top)
            totals.append(sum(jnp.sum(jnp.exp2(part - top[None]), axis=0) for part in parts))
        for (q_at, _, _), top, total in zip(todo, tops, totals):
            rows = rows_at(q_at, 8)
            old = ms[rows, :]
            new = jnp.maximum(old, top)
            ls[rows, :] = ls[rows, :] * jnp.exp2(old - new) + total * jnp.exp2(top - new)
            ms[rows, :] = new
        return carry

    lax.fori_loop(0, steps // TURN, turn, 0)
    for i in range(QSPANS):
        run_max, run_sum = ms[part_slice(i, 8), :], ls[part_slice(i, 8), :]
        old_max, old_sum = before[i : i + 1, :], before[QSPANS + i : QSPANS + i + 1, :]
        top = jnp.maximum(jnp.max(run_max, axis=0, keepdims=True), old_max)
        total = jnp.sum(run_sum * jnp.exp2(run_max - top), axis=0, keepdims=True)
        out_ref[i : i + 1, :] = top
        out_ref[QSPANS + i : QSPANS + i + 1, :] = total + old_sum * jnp.exp2(old_max - top)


def grads_kernel(spans, steps, last, *refs):
    meta, kv_ref, *queries = refs[: 2 + SHARE]
    grads, stats, refs = refs[6:10], refs[10:14], refs[14:]
    if last:
        dq_before, dkv_ref, *dq_refs = refs[: 2 + SHARE]
        kvin, qin, gin, dkv, own, others, ks, vs, kt, dka, dva, qs, gs, lt, dqa, sems = refs[6:]
    else:
        dkv_ref, dq_ref, kvin, qin, gin, dkv, ks, vs, kt, dka, dva, qs, gs, lt, dqa, sems = refs
    copies = load_all(
        (kv_ref, *queries, *grads),
        (kvin, *[qin.at[n] for n in range(SHARE)], *[gin.at[n] for n in range(SHARE)]),
        sems,
    )
    if last:
        copies.append(pltpu.make_async_copy(dq_before, dqa, sems.at[2 * SHARE + 1]))
        copies[-1].start()
    else:
        dqa[...] = jnp.zeros_like(dqa)
    dka[...] = jnp.zeros_like(dka)
    dva[...] = jnp.zeros_like(dva)
    vs[:, HEAD:] = jnp.full((spans * SPAN, HEAD), -1.0, BF16)
    copies[0].wait()

    def copy_span(n, carry):
        rows = rows_at(n, SPAN)
        ks[rows, :] = kvin[span_rows(meta[n], 0), :]
        vs[rows, :HEAD] = kvin[span_rows(meta[n], 1), :]
        return carry

    lax.fori_loop(0, spans, copy_span, 0, unroll=8)
    for block in range(spans // SUBS):
        kt[part_slice(block, HEAD), :] = ks[part_slice(block, BLOCK), :].astype(F32).T.astype(BF16)
    pattern = mask_pattern()
    lane = lax.broadcasted_iota(jnp.int32, (SPAN, HEAD), 1)
    for copy in copies[1:]:
        copy.wait()
    for i in range(QSPANS):
        slot, half = i // 2, i % 2
        tokens = span_slice(half)
        extra = gin[slot, tokens, WIDTH:].astype(F32)
        for h in range(GROUP):
            rows = part_slice(i * GROUP + h, SPAN)
            qs[rows, :] = qin[slot, tokens, head_cols(h)]
            gs[rows, :HEAD] = gin[slot, tokens, head_cols(h)]
            ours = jnp.logical_and(lane % GROUP == h, lane < 3 * GROUP)
            gs[rows, HEAD:] = jnp.where(ours, extra, 0.0).astype(BF16)
        tops, sums = [], []
        for shift in range(SHARE):
            row = ((slot - shift) % SHARE) * 2 + half
            tops.append(stats[shift][row : row + 1, :])
            sums.append(stats[shift][QSPANS + row : QSPANS + row + 1, :])
        top = functools.reduce(jnp.maximum, tops)
        total = sum(s * jnp.exp2(t - top) for s, t in zip(sums, tops))
        lt[part_slice(i, 8), :] = jnp.broadcast_to(top + jnp.log(total) * LOG2E, (8, COLS))

    def turn(index, carry):
        todo = [step_of(meta, spans, index * TURN + u) for u in range(TURN)]
        key_rows = [rows_at(block, BLOCK) for _, block, _ in todo]
        query_rows = [rows_at(q_at, COLS) for q_at, _, _ in todo]
        scores, grad_probs = [], []
        for kr, qr in zip(key_rows, query_rows):
            scores.append(dot(ks[kr, :], qs[qr, :], 1, 1))
            grad_probs.append(dot(vs[kr, :], gs[qr, :], 1, 1))
        probs, grad_scores = [], []
        for u, (q_at, block, query_pos) in enumerate(todo):
            log_total = lt[rows_at(q_at, 8), :][None]
            low, low_grad = [], []
            for sub in range(SUBS):
                gap = (query_pos - meta[spans + block * SUBS + sub]) * SPAN
                rows = part_slice(sub, SPAN)
                part = scores[u][rows].reshape(SPAN // 8, 8, COLS) * SCALE2 - log_total
                part = jnp.where(pattern <= gap, jnp.exp2(part.reshape(SPAN, COLS)), 0.0)
                low.append(part.astype(BF16))
                low_grad.append((part * grad_probs[u][rows]).astype(BF16))
            probs.append(jnp.concatenate(low, axis=0))
            grad_scores.append(jnp.concatenate(low_grad, axis=0))
        to_value, to_key, to_query = [], [], []
        for u, (_, block, _) in enumerate(todo):
            to_value.append(dot(probs[u], gs[query_rows[u], :HEAD], 1, 0))
            to_key.append(dot(grad_scores[u], qs[query_rows[u], :], 1, 0))
            to_query.append(dot(kt[rows_at(block, HEAD), :], grad_scores[u], 1, 0))
        for u, (q_at, _, _) in enumerate(todo):
            dva[key_rows[u], :] += to_value[u]
            dka[key_rows[u], :] += to_key[u]
            dqa[rows_at(q_at, HEAD), :] += to_query[u]
        return carry

    lax.fori_loop(0, steps // TURN, turn, 0)
    copies = []
    if last:
        for slot in reversed(range(SHARE)):
            out = own if slot == 0 else others.at[slot - 1]
            for half in range(2):
                full = dqa[part_slice(2 * slot + half, HEAD), :].T * SCALE
                for h in range(GROUP):
                    out[span_slice(half), head_cols(h)] = full[part_slice(h, SPAN)].astype(out.dtype)
            copies.append(pltpu.make_async_copy(out, dq_refs[slot], sems.at[slot]))
            copies[-1].start()
    else:
        copies.append(pltpu.make_async_copy(dqa, dq_ref, sems.at[0]))
        copies[-1].start()

    def place_span(n, carry):
        rows = rows_at(n, SPAN)
        dkv[span_rows(meta[n], 0), :] = (dka[rows, :] * SCALE).astype(dkv.dtype)
        dkv[span_rows(meta[n], 1), :] = dva[rows, :].astype(dkv.dtype)
        return carry

    lax.fori_loop(0, spans, place_span, 0, unroll=8)
    copies.append(pltpu.make_async_copy(dkv, dkv_ref, sems.at[SHARE]))
    copies[-1].start()
    for copy in copies:
        copy.wait()


def query_part_kernel(peers, d0, d1, d2, d3, w_ref, out_ref):
    query = d0[...]
    for part in (d1, d2, d3):
        query = query + part[...].astype(F32)
    query = query.astype(BF16)
    feats = out_ref.shape[2]
    for s in range(out_ref.shape[0]):
        out_ref[s, :, :] = dot(query, w_ref[rows_at(peers[s], feats), :], 1, 1)


def project_kernel(peers, dkv_ref, part_ref, wk_ref, wv_ref, o0, o1, o2, o3):
    tokens, feats = o0.shape
    sums = jnp.zeros((2 * tokens, HEAD), F32)
    for member in range(dkv_ref.shape[0] // (2 * tokens)):
        sums = sums + dkv_ref[part_slice(member, 2 * tokens), :].astype(F32)
    sums = sums.astype(BF16)
    for s, out in enumerate((o0, o1, o2, o3)):
        rows = rows_at(peers[s], feats)
        total = part_ref[s, :, :] + dot(sums[:tokens], wk_ref[rows, :], 1, 1)
        total = total + dot(sums[tokens:], wv_ref[rows, :], 1, 1)
        out[...] = total.astype(out.dtype)


VMEM = pl.BlockSpec(memory_space=pltpu.VMEM)
SMEM = pl.BlockSpec(memory_space=pltpu.SMEM)
HBM = pl.BlockSpec(memory_space=pltpu.HBM)
LARGE = pltpu.CompilerParams(vmem_limit_bytes=60 * 1024 * 1024)
SMALL = pltpu.CompilerParams(vmem_limit_bytes=16 * 1024 * 1024)


def shape(dims, dtype):
    return jax.ShapeDtypeStruct(dims, dtype)


def step_tables(span_pos, side, member, share, members, steps):
    spans = 2 * members
    cut = span_pos.reshape(SIDES, members, SHARE, 2)
    key_pos = lax.dynamic_slice_in_dim(cut, share, 1, axis=2).reshape(SIDES, spans)
    key_pos = jnp.where(side == 0, key_pos, key_pos[::-1])
    ids = jnp.arange(spans, dtype=jnp.int32)
    rank = jnp.sum((key_pos[:, None, :] < key_pos[:, :, None]).astype(jnp.int32), axis=2)
    placed = rank[:, None, :] == ids[None, :, None]
    order = jnp.sum(jnp.where(placed, ids[None, None, :], 0), axis=2)
    sorted_pos = jnp.sum(jnp.where(placed, key_pos[:, None, :], 0), axis=2)
    slots = jnp.arange(SHARE, dtype=jnp.int32)
    source = ((side * members + member) * SHARE + (share + SHARE - slots) % SHARE) * 2
    places = jnp.arange(span_pos.shape[0], dtype=jnp.int32)
    query_pos = [
        jnp.sum(jnp.where(places[None, :] == source[:, None] + h, span_pos[None, :], 0), axis=1)
        for h in range(2)
    ]
    blocks = [
        (jnp.sum((key_pos[:, None, :] <= qp[None, :, None]).astype(jnp.int32), axis=2) + SUBS - 1)
        // SUBS
        for qp in query_pos
    ]
    first, other = blocks[0][:, :, None], blocks[1][:, :, None]
    at = jnp.arange(steps // SHARE, dtype=jnp.int32)[None, None, :]
    second = at >= first
    block = jnp.where(second, at - first, at)
    used = jnp.logical_or(jnp.logical_not(second), block < other)
    q_at = jnp.where(second, 1, 0) + 2 * slots[None, :, None]
    pos = jnp.where(second, query_pos[1][None, :, None], query_pos[0][None, :, None])
    table = jnp.stack([q_at, jnp.where(used, block, 0), jnp.where(used, pos, -1)], axis=3)
    return jnp.concatenate([order, sorted_pos, table.reshape(SIDES, -1)], axis=1)


def local(q, k, v, o, g, w_query, key_weight, value_weight, span_pos):
    tokens = q.shape[0]
    cycle = lax.axis_size("ctx")
    tp_size = lax.axis_size("tp")
    members = cycle // SHARE // SIDES
    spans = 2 * members
    half_rows = 2 * spans * SPAN
    steps = SHARE * ((spans + 1 + 2 * (SUBS - 1)) // SUBS)
    index = lax.axis_index("ctx")
    share, member, side = index % SHARE, index // SHARE % members, index // (SHARE * members)

    def device(side_at, member_at, share_at):
        return (side_at % SIDES * members + member_at) * SHARE + share_at % SHARE

    places = [(a, b, c) for a in range(SIDES) for b in range(members) for c in range(SHARE)]
    key_groups = [
        [device(a, b, c) for b in range(members)] for a in range(SIDES) for c in range(SHARE)
    ]

    def exchanged(array):
        return lax.all_to_all(array, "ctx", 0, 0, tiled=True, axis_index_groups=key_groups)

    def shifted(array, by):
        return lax.ppermute(array, "ctx", [(device(a, b, c), device(a, b, c + by)) for a, b, c in places])

    def crossed(array):
        return lax.ppermute(array, "ctx", [(device(a, b, c), device(a + 1, b, c)) for a, b, c in places])

    copies = pl.pallas_call(
        tile_kernel,
        out_shape=shape((half_rows, HEAD), BF16),
        in_specs=[VMEM] * 2,
        out_specs=VMEM,
        name="tile",
    )(k, v)
    kv_own = exchanged(copies)
    queries = [q] + [shifted(q, s) for s in range(1, SHARE)]
    packed = pl.pallas_call(
        pack_kernel,
        out_shape=shape((tokens, WIDTH + HEAD), BF16),
        in_specs=[VMEM] * 2,
        out_specs=VMEM,
        name="pack",
    )(g, o)
    packs = [packed] + [shifted(packed, s) for s in range(1, SHARE)]
    meta = step_tables(span_pos, side, member, share, members, steps)
    meta_own, meta_other = meta[0], meta[1]
    kv_other = crossed(kv_own)

    def stats_of(table, kv, before):
        return pl.pallas_call(
            functools.partial(stats_kernel, spans, steps),
            out_shape=shape((2 * QSPANS, COLS), F32),
            in_specs=[SMEM] + [HBM] * 5 + [VMEM],
            out_specs=VMEM,
            scratch_shapes=[
                pltpu.VMEM((half_rows, HEAD), BF16),
                pltpu.VMEM((SHARE, tokens, WIDTH), BF16),
                pltpu.VMEM((spans * SPAN, HEAD), BF16),
                pltpu.VMEM((QSPANS * COLS, HEAD), BF16),
                pltpu.VMEM((QSPANS * 8, COLS), F32),
                pltpu.VMEM((QSPANS * 8, COLS), F32),
                pltpu.SemaphoreType.DMA((5,)),
            ],
            compiler_params=LARGE,
            cost_estimate=pl.CostEstimate(
                flops=1 << 30, bytes_accessed=1 << 22, transcendentals=1 << 22
            ),
            name="stats",
        )(table, kv, *queries, before)

    empty = jnp.concatenate(
        [jnp.full((QSPANS, COLS), NEG, F32), jnp.zeros((QSPANS, COLS), F32)], axis=0
    )
    stats = stats_of(meta_other, kv_other, stats_of(meta_own, kv_own, empty))
    all_stats = [stats] + [shifted(stats, s) for s in range(1, SHARE)]

    def grads_of(table, kv, last, extra_in, outs, extra_scratch):
        return pl.pallas_call(
            functools.partial(grads_kernel, spans, steps, last),
            out_shape=outs,
            in_specs=[SMEM] + [HBM] * 9 + [VMEM] * 4 + [HBM] * len(extra_in),
            out_specs=[HBM] * len(outs),
            scratch_shapes=[
                pltpu.VMEM((half_rows, HEAD), BF16),
                pltpu.VMEM((SHARE, tokens, WIDTH), BF16),
                pltpu.VMEM((SHARE, tokens, WIDTH + HEAD), BF16),
                pltpu.VMEM((half_rows, HEAD), outs[0].dtype),
                *extra_scratch,
                pltpu.VMEM((spans * SPAN, HEAD), BF16),
                pltpu.VMEM((spans * SPAN, 2 * HEAD), BF16),
                pltpu.VMEM((spans // SUBS * HEAD, BLOCK), BF16),
                pltpu.VMEM((spans * SPAN, HEAD), F32),
                pltpu.VMEM((spans * SPAN, HEAD), F32),
                pltpu.VMEM((QSPANS * COLS, HEAD), BF16),
                pltpu.VMEM((QSPANS * COLS, 2 * HEAD), BF16),
                pltpu.VMEM((QSPANS * 8, COLS), F32),
                pltpu.VMEM((QSPANS * HEAD, COLS), F32),
                pltpu.SemaphoreType.DMA((2 * SHARE + 2,)),
            ],
            compiler_params=LARGE,
            cost_estimate=pl.CostEstimate(
                flops=1 << 31, bytes_accessed=1 << 23, transcendentals=1 << 22
            ),
            name="grads",
        )(table, kv, *queries, *packs, *all_stats, *extra_in)

    dkv_other, dq_before = grads_of(
        meta_other,
        kv_other,
        False,
        [],
        [shape((half_rows, HEAD), BF16), shape((QSPANS * HEAD, COLS), F32)],
        [],
    )
    dkv_crossed = crossed(dkv_other)
    dkv_own, *dqs = grads_of(
        meta_own,
        kv_own,
        True,
        [dq_before],
        [shape((half_rows, HEAD), F32), shape((tokens, WIDTH), F32)]
        + [shape((tokens, WIDTH), BF16)] * (SHARE - 1),
        [pltpu.VMEM((tokens, WIDTH), F32), pltpu.VMEM((SHARE - 1, tokens, WIDTH), BF16)],
    )
    dkv_parts = exchanged((dkv_own + dkv_crossed.astype(F32)).astype(BF16))
    dq_parts = [shifted(dqs[s], -s) for s in range(1, SHARE)]
    peers = (lax.axis_index("tp") + jnp.arange(tp_size, dtype=jnp.int32)) % tp_size
    feats = w_query.shape[0] // tp_size
    query_part = pl.pallas_call(
        query_part_kernel,
        out_shape=shape((tp_size, tokens, feats), F32),
        in_specs=[SMEM] + [VMEM] * 5,
        out_specs=VMEM,
        compiler_params=SMALL,
        name="query_part",
    )(peers, dqs[0], *dq_parts, w_query)
    own, *pieces = pl.pallas_call(
        project_kernel,
        out_shape=[shape((tokens, feats), F32)] + [shape((tokens, feats), BF16)] * (tp_size - 1),
        in_specs=[SMEM] + [VMEM] * 4,
        out_specs=[VMEM] * tp_size,
        compiler_params=SMALL,
        name="project",
    )(peers, dkv_parts, query_part, key_weight, value_weight)
    for s in range(1, tp_size):
        pairs = [(d, (d + s) % tp_size) for d in range(tp_size)]
        own = own + lax.ppermute(pieces[s - 1], "tp", pairs).astype(F32)
    return own.astype(BF16)


def solution(mesh):
    row, col = P("ctx", "tp"), P(None, "tp")
    in_specs = (row, row, row, row, row, col, col, col, P())
    return jax.shard_map(local, mesh=mesh, in_specs=in_specs, out_specs=row, check_vma=False)
```

```python
import functools
import math

import jax
import jax.numpy as jnp
from jax import lax
from jax.experimental import pallas as pl
from jax.experimental.pallas import tpu as pltpu
from jax.sharding import PartitionSpec as P

HEAD = 128
SPAN = 64
GROUP = 4
SHARE = 4
SIDES = 2
SUBS = 4
BLOCK = SUBS * SPAN
COLS = GROUP * SPAN
WIDTH = GROUP * HEAD
QSPANS = 2 * SHARE
STATS = 3 * QSPANS
SCALE = HEAD ** (-0.5)
LOG2E = math.log2(math.e)
SCALE2 = SCALE * LOG2E
NEG = -1e30
F32 = jnp.float32
BF16 = jnp.bfloat16


def dot(left, right, left_dim, right_dim):
    return lax.dot_general(
        left, right, (((left_dim,), (right_dim,)), ((), ())), preferred_element_type=F32
    )


def rows_at(index, size):
    return pl.ds(pl.multiple_of(index * size, size), size)


def span_rows(slot, value):
    return rows_at(slot // 2 * 4 + slot % 2 + 2 * value, SPAN)


def load_all(sources, buffers, sems):
    copies = [
        pltpu.make_async_copy(source, buffer, sems.at[n])
        for n, (source, buffer) in enumerate(zip(sources, buffers))
    ]
    for copy in copies:
        copy.start()
    return copies


def head_cols(head, first=0):
    return slice(first + head * HEAD, first + (head + 1) * HEAD)


def span_slice(half):
    return slice(half * SPAN, (half + 1) * SPAN)


def part_slice(index, size):
    return slice(index * size, (index + 1) * size)


def tile_kernel(k_ref, v_ref, out_ref):
    tokens = k_ref.shape[0]
    for member in range(out_ref.shape[0] // (2 * tokens)):
        out_ref[part_slice(2 * member, tokens), :] = k_ref[...]
        out_ref[part_slice(2 * member + 1, tokens), :] = v_ref[...]


def pack_kernel(q_ref, g_ref, o_ref, out_ref, start_ref):
    start_ref[:QSPANS, :] = jnp.full((QSPANS, COLS), NEG, F32)
    start_ref[QSPANS:, :] = jnp.zeros((STATS - QSPANS, COLS), F32)
    ones = jnp.ones((8, HEAD), BF16)
    for half in range(2):
        products = []
        for h in range(GROUP):
            rows, tokens = part_slice(half * GROUP + h, SPAN), span_slice(half)
            grad = g_ref[tokens, head_cols(h)]
            out_ref[rows, :HEAD] = q_ref[tokens, head_cols(h)]
            out_ref[rows, HEAD:] = grad
            products.append(grad.astype(F32) * o_ref[tokens, head_cols(h)].astype(F32))
        rest = jnp.concatenate(products, axis=0)
        delta = jnp.zeros((8, COLS), F32)
        for _ in range(3):
            part = rest.astype(BF16)
            delta = delta + dot(ones, part, 1, 1)
            rest = rest - part.astype(F32)
        start_ref[2 * QSPANS + half : 2 * QSPANS + half + 1, :] = delta[:1]


def mask_pattern():
    row = lax.broadcasted_iota(jnp.int32, (SPAN, COLS), 0)
    col = lax.broadcasted_iota(jnp.int32, (SPAN, COLS), 1)
    return row - col % SPAN


def slot_steps(meta, spans, steps, slot):
    count = steps // SHARE
    starts = [2 * spans + 3 * (slot * count + n) for n in range(count)]
    return [(meta[at], meta[at + 1], meta[at + 2]) for at in starts]


def slot_rows(ref, slot):
    return ref.at[part_slice(slot, 2 * COLS)]


def stats_kernel(spans, steps, meta, k_ref, b0, b1, b2, b3, before, out_ref, kin, ks, qs, ms, ls, sems):
    copies = load_all(
        (k_ref, *[b.at[:, :HEAD] for b in (b0, b1, b2, b3)]),
        (kin, *[slot_rows(qs, n) for n in range(SHARE)]),
        sems,
    )
    copies[0].wait()

    def copy_span(n, carry):
        ks[rows_at(n, SPAN), :] = kin[rows_at(meta[n], SPAN), :]
        return carry

    lax.fori_loop(0, spans, copy_span, 0, unroll=8)
    ms[...] = jnp.full_like(ms, NEG)
    ls[...] = jnp.zeros_like(ls)
    pattern = mask_pattern()
    for slot in range(SHARE):
        copies[1 + slot].wait()
        todo = slot_steps(meta, spans, steps, slot)
        scores = [
            dot(ks[rows_at(block, BLOCK), :], qs[rows_at(q_at, COLS), :], 1, 1)
            for q_at, block, _ in todo
        ]
        tops, totals = [], []
        for (_, block, query_pos), score in zip(todo, scores):
            parts = []
            for sub in range(SUBS):
                gap = (query_pos - meta[spans + block * SUBS + sub]) * SPAN
                part = jnp.where(pattern <= gap, score[part_slice(sub, SPAN)] * SCALE2, NEG)
                parts.append(part.reshape(SPAN // 8, 8, COLS))
            top = functools.reduce(jnp.maximum, [jnp.max(part, axis=0) for part in parts])
            tops.append(top)
            totals.append(sum(jnp.sum(jnp.exp2(part - top[None]), axis=0) for part in parts))
        for (q_at, _, _), top, total in zip(todo, tops, totals):
            rows = rows_at(q_at, 8)
            old = ms[rows, :]
            new = jnp.maximum(old, top)
            ls[rows, :] = ls[rows, :] * jnp.exp2(old - new) + total * jnp.exp2(top - new)
            ms[rows, :] = new
    out_ref[2 * QSPANS :, :] = before[2 * QSPANS :, :]
    for i in range(QSPANS):
        run_max, run_sum = ms[part_slice(i, 8), :], ls[part_slice(i, 8), :]
        old_max, old_sum = before[i : i + 1, :], before[QSPANS + i : QSPANS + i + 1, :]
        top = jnp.maximum(jnp.max(run_max, axis=0, keepdims=True), old_max)
        total = jnp.sum(run_sum * jnp.exp2(run_max - top), axis=0, keepdims=True)
        out_ref[i : i + 1, :] = top
        out_ref[QSPANS + i : QSPANS + i + 1, :] = total + old_sum * jnp.exp2(old_max - top)


def grads_kernel(spans, steps, last, *refs):
    meta, k_ref, v_ref = refs[:3]
    blocks, stats, refs = refs[3:7], refs[7:11], refs[11:]
    if last:
        dq_before, dkv_ref, *dq_refs = refs[: 2 + SHARE]
        kin, vin, dkv, own, others, ks, vs, kt, dka, dva, qs, gs, lt, dl, dqa, sems = refs[6:]
    else:
        dkv_ref, dq_ref, kin, vin, dkv, ks, vs, kt, dka, dva, qs, gs, lt, dl, dqa, sems = refs
    copies = load_all(
        (k_ref, v_ref, *[b.at[:, :HEAD] for b in blocks], *[b.at[:, HEAD:] for b in blocks]),
        (
            kin,
            vin,
            *[slot_rows(qs, n) for n in range(SHARE)],
            *[slot_rows(gs, n) for n in range(SHARE)],
        ),
        sems,
    )
    if last:
        before = [dq_before.at[part_slice(n, 2 * HEAD)] for n in range(SHARE)]
        targets = [dqa.at[part_slice(n, 2 * HEAD)] for n in range(SHARE)]
        copies += load_all(before, targets, sems.at[2 * SHARE + 2 :])
    else:
        dqa[...] = jnp.zeros_like(dqa)
    dka[...] = jnp.zeros_like(dka)
    dva[...] = jnp.zeros_like(dva)
    copies[0].wait()
    copies[1].wait()

    def copy_span(n, carry):
        rows = rows_at(n, SPAN)
        ks[rows, :] = kin[rows_at(meta[n], SPAN), :]
        vs[rows, :] = vin[rows_at(meta[n], SPAN), :]
        return carry

    lax.fori_loop(0, spans, copy_span, 0, unroll=8)
    for block in range(spans // SUBS):
        kt[part_slice(block, HEAD), :] = ks[part_slice(block, BLOCK), :].astype(F32).T.astype(BF16)
    pattern = mask_pattern()
    for i in range(QSPANS):
        slot, half = i // 2, i % 2
        delta = stats[slot][2 * QSPANS + half : 2 * QSPANS + half + 1, :]
        dl[part_slice(i, 8), :] = jnp.broadcast_to(delta, (8, COLS))
        tops, sums = [], []
        for shift in range(SHARE):
            row = ((slot - shift) % SHARE) * 2 + half
            tops.append(stats[shift][row : row + 1, :])
            sums.append(stats[shift][QSPANS + row : QSPANS + row + 1, :])
        top = functools.reduce(jnp.maximum, tops)
        total = sum(s * jnp.exp2(t - top) for s, t in zip(sums, tops))
        lt[part_slice(i, 8), :] = jnp.broadcast_to(top + jnp.log(total) * LOG2E, (8, COLS))
    stores = []
    for slot in range(SHARE):
        for copy in copies[2 + slot :: SHARE]:
            copy.wait()
        todo = slot_steps(meta, spans, steps, slot)
        key_rows = [rows_at(block, BLOCK) for _, block, _ in todo]
        query_rows = [rows_at(q_at, COLS) for q_at, _, _ in todo]
        scores, grad_probs = [], []
        for kr, qr in zip(key_rows, query_rows):
            scores.append(dot(ks[kr, :], qs[qr, :], 1, 1))
            grad_probs.append(dot(vs[kr, :], gs[qr, :], 1, 1))
        probs, grad_scores = [], []
        for u, (q_at, block, query_pos) in enumerate(todo):
            log_total, delta = lt[rows_at(q_at, 8), :][None], dl[rows_at(q_at, 8), :][None]
            low, low_grad = [], []
            for sub in range(SUBS):
                gap = (query_pos - meta[spans + block * SUBS + sub]) * SPAN
                rows = part_slice(sub, SPAN)
                part = scores[u][rows].reshape(SPAN // 8, 8, COLS) * SCALE2 - log_total
                part = jnp.where(pattern <= gap, jnp.exp2(part.reshape(SPAN, COLS)), 0.0)
                low.append(part.astype(BF16))
                change = grad_probs[u][rows].reshape(SPAN // 8, 8, COLS) - delta
                low_grad.append((part * change.reshape(SPAN, COLS)).astype(BF16))
            probs.append(jnp.concatenate(low, axis=0))
            grad_scores.append(jnp.concatenate(low_grad, axis=0))
        to_value, to_key, to_query = [], [], []
        for u, (_, block, _) in enumerate(todo):
            to_value.append(dot(probs[u], gs[query_rows[u], :], 1, 0))
            to_key.append(dot(grad_scores[u], qs[query_rows[u], :], 1, 0))
            to_query.append(dot(kt[rows_at(block, HEAD), :], grad_scores[u], 1, 0))
        for u, (q_at, _, _) in enumerate(todo):
            dva[key_rows[u], :] += to_value[u]
            dka[key_rows[u], :] += to_key[u]
            dqa[rows_at(q_at, HEAD), :] += to_query[u]
        store_sem = sems.at[3 * SHARE + 2 + slot]
        if last:
            out = own if slot == 0 else others.at[slot - 1]
            for half in range(2):
                full = dqa[part_slice(2 * slot + half, HEAD), :].T * SCALE
                for h in range(GROUP):
                    out[span_slice(half), head_cols(h)] = full[part_slice(h, SPAN)].astype(out.dtype)
            stores.append(pltpu.make_async_copy(out, dq_refs[slot], store_sem))
        else:
            rows = part_slice(slot, 2 * HEAD)
            stores.append(pltpu.make_async_copy(dqa.at[rows], dq_ref.at[rows], store_sem))
        stores[-1].start()

    def place_span(n, carry):
        rows = rows_at(n, SPAN)
        dkv[span_rows(meta[n], 0), :] = (dka[rows, :] * SCALE).astype(dkv.dtype)
        dkv[span_rows(meta[n], 1), :] = dva[rows, :].astype(dkv.dtype)
        return carry

    lax.fori_loop(0, spans, place_span, 0, unroll=8)
    stores.append(pltpu.make_async_copy(dkv, dkv_ref, sems.at[4 * SHARE + 2]))
    stores[-1].start()
    for store in stores:
        store.wait()


def project_kernel(
    peers, d0, d1, d2, d3, dkv_ref, wk_ref, wv_ref, wq_ref, o0, o1, o2, o3,
    own, others, dkv, wk, wv, sems,
):
    tokens, feats = o0.shape
    copies = load_all(
        (d0, d1, d2, d3, dkv_ref, wk_ref, wv_ref),
        (own, *[others.at[n] for n in range(SHARE - 1)], dkv, wk, wv),
        sems,
    )
    for copy in copies[:SHARE]:
        copy.wait()
    query = own[...]
    for n in range(SHARE - 1):
        query = query + others[n].astype(F32)
    query = query.astype(BF16)
    rows = [rows_at(peers[s], feats) for s in range(SHARE)]
    totals = [dot(query, wq_ref[at, :], 1, 1) for at in rows]
    copies[SHARE].wait()
    sums = jnp.zeros((2 * tokens, HEAD), F32)
    for member in range(dkv.shape[0] // (2 * tokens)):
        sums = sums + dkv[part_slice(member, 2 * tokens), :].astype(F32)
    sums = sums.astype(BF16)
    for copy in copies[SHARE + 1 :]:
        copy.wait()
    for at, total, out in zip(rows, totals, (o0, o1, o2, o3)):
        total = total + dot(sums[:tokens], wk[at, :], 1, 1)
        total = total + dot(sums[tokens:], wv[at, :], 1, 1)
        out[...] = total.astype(out.dtype)


VMEM = pl.BlockSpec(memory_space=pltpu.VMEM)
SMEM = pl.BlockSpec(memory_space=pltpu.SMEM)
HBM = pl.BlockSpec(memory_space=pltpu.HBM)
LARGE = pltpu.CompilerParams(vmem_limit_bytes=60 * 1024 * 1024)
SMALL = pltpu.CompilerParams(vmem_limit_bytes=16 * 1024 * 1024)


def shape(dims, dtype):
    return jax.ShapeDtypeStruct(dims, dtype)


def step_tables(span_pos, side, member, share, members, steps):
    spans = 2 * members
    cut = span_pos.reshape(SIDES, members, SHARE, 2)
    key_pos = lax.dynamic_slice_in_dim(cut, share, 1, axis=2).reshape(SIDES, spans)
    key_pos = jnp.where(side == 0, key_pos, key_pos[::-1])
    ids = jnp.arange(spans, dtype=jnp.int32)
    rank = jnp.sum((key_pos[:, None, :] < key_pos[:, :, None]).astype(jnp.int32), axis=2)
    placed = rank[:, None, :] == ids[None, :, None]
    order = jnp.sum(jnp.where(placed, ids[None, None, :], 0), axis=2)
    sorted_pos = jnp.sum(jnp.where(placed, key_pos[:, None, :], 0), axis=2)
    slots = jnp.arange(SHARE, dtype=jnp.int32)
    source = ((side * members + member) * SHARE + (share + SHARE - slots) % SHARE) * 2
    places = jnp.arange(span_pos.shape[0], dtype=jnp.int32)
    query_pos = [
        jnp.sum(jnp.where(places[None, :] == source[:, None] + h, span_pos[None, :], 0), axis=1)
        for h in range(2)
    ]
    blocks = [
        (jnp.sum((key_pos[:, None, :] <= qp[None, :, None]).astype(jnp.int32), axis=2) + SUBS - 1)
        // SUBS
        for qp in query_pos
    ]
    first, other = blocks[0][:, :, None], blocks[1][:, :, None]
    at = jnp.arange(steps // SHARE, dtype=jnp.int32)[None, None, :]
    second = at >= first
    block = jnp.where(second, at - first, at)
    used = jnp.logical_or(jnp.logical_not(second), block < other)
    q_at = jnp.where(second, 1, 0) + 2 * slots[None, :, None]
    pos = jnp.where(second, query_pos[1][None, :, None], query_pos[0][None, :, None])
    table = jnp.stack([q_at, jnp.where(used, block, 0), jnp.where(used, pos, -1)], axis=3)
    return jnp.concatenate([order, sorted_pos, table.reshape(SIDES, -1)], axis=1)


def local(q, k, v, o, g, w_query, key_weight, value_weight, span_pos):
    tokens = q.shape[0]
    cycle = lax.axis_size("ctx")
    tp_size = lax.axis_size("tp")
    members = cycle // SHARE // SIDES
    spans = 2 * members
    half_rows = 2 * spans * SPAN
    steps = SHARE * ((spans + 1 + 2 * (SUBS - 1)) // SUBS)
    index = lax.axis_index("ctx")
    share, member, side = index % SHARE, index // SHARE % members, index // (SHARE * members)

    def device(side_at, member_at, share_at):
        return (side_at % SIDES * members + member_at) * SHARE + share_at % SHARE

    places = [(a, b, c) for a in range(SIDES) for b in range(members) for c in range(SHARE)]
    key_groups = [
        [device(a, b, c) for b in range(members)] for a in range(SIDES) for c in range(SHARE)
    ]

    def exchanged(array):
        return lax.all_to_all(array, "ctx", 0, 0, tiled=True, axis_index_groups=key_groups)

    def shifted(array, by):
        return lax.ppermute(array, "ctx", [(device(a, b, c), device(a, b, c + by)) for a, b, c in places])

    def crossed(array):
        return lax.ppermute(array, "ctx", [(device(a, b, c), device(a + 1, b, c)) for a, b, c in places])

    copies = pl.pallas_call(
        tile_kernel,
        out_shape=shape((half_rows, HEAD), BF16),
        in_specs=[VMEM] * 2,
        out_specs=VMEM,
        name="tile",
    )(k, v)
    q, copies = lax.optimization_barrier((q, copies))
    block, start = pl.pallas_call(
        pack_kernel,
        out_shape=[shape((2 * COLS, 2 * HEAD), BF16), shape((STATS, COLS), F32)],
        in_specs=[VMEM] * 3,
        out_specs=[VMEM] * 2,
        cost_estimate=pl.CostEstimate(flops=1 << 35, bytes_accessed=1 << 20, transcendentals=0),
        name="pack",
    )(q, g, o)
    kv_own = exchanged(copies)
    blocks = [block] + [shifted(block, s) for s in range(1, SHARE)]
    meta = step_tables(span_pos, side, member, share, members, steps)
    meta_own, meta_other = meta[0], meta[1]
    sides = kv_own.reshape(members, 2, tokens, HEAD)
    k_own, v_own = [sides[:, n].reshape(spans * SPAN, HEAD) for n in range(2)]
    k_other = crossed(k_own)

    def stats_of(table, keys, before):
        return pl.pallas_call(
            functools.partial(stats_kernel, spans, steps),
            out_shape=shape((STATS, COLS), F32),
            in_specs=[SMEM] + [HBM] * 5 + [VMEM],
            out_specs=VMEM,
            scratch_shapes=[
                pltpu.VMEM((spans * SPAN, HEAD), BF16),
                pltpu.VMEM((spans * SPAN, HEAD), BF16),
                pltpu.VMEM((QSPANS * COLS, HEAD), BF16),
                pltpu.VMEM((QSPANS * 8, COLS), F32),
                pltpu.VMEM((QSPANS * 8, COLS), F32),
                pltpu.SemaphoreType.DMA((5,)),
            ],
            compiler_params=LARGE,
            cost_estimate=pl.CostEstimate(
                flops=1 << 30, bytes_accessed=1 << 22, transcendentals=1 << 22
            ),
            name="stats",
        )(table, keys, *blocks, before)

    stats_own, v_late = lax.optimization_barrier((stats_of(meta_own, k_own, start), v_own))
    v_other = crossed(v_late)
    stats = stats_of(meta_other, k_other, stats_own)
    all_stats = [stats] + [shifted(stats, s) for s in range(1, SHARE)]

    def grads_of(table, keys, values, last, extra_in, outs, extra_scratch):
        return pl.pallas_call(
            functools.partial(grads_kernel, spans, steps, last),
            out_shape=outs,
            in_specs=[SMEM] + [HBM] * 6 + [VMEM] * 4 + [HBM] * len(extra_in),
            out_specs=[HBM] * len(outs),
            scratch_shapes=[
                pltpu.VMEM((spans * SPAN, HEAD), BF16),
                pltpu.VMEM((spans * SPAN, HEAD), BF16),
                pltpu.VMEM((half_rows, HEAD), outs[0].dtype),
                *extra_scratch,
                pltpu.VMEM((spans * SPAN, HEAD), BF16),
                pltpu.VMEM((spans * SPAN, HEAD), BF16),
                pltpu.VMEM((spans // SUBS * HEAD, BLOCK), BF16),
                pltpu.VMEM((spans * SPAN, HEAD), F32),
                pltpu.VMEM((spans * SPAN, HEAD), F32),
                pltpu.VMEM((QSPANS * COLS, HEAD), BF16),
                pltpu.VMEM((QSPANS * COLS, HEAD), BF16),
                pltpu.VMEM((QSPANS * 8, COLS), F32),
                pltpu.VMEM((QSPANS * 8, COLS), F32),
                pltpu.VMEM((QSPANS * HEAD, COLS), F32),
                pltpu.SemaphoreType.DMA((4 * SHARE + 3,)),
            ],
            compiler_params=LARGE,
            cost_estimate=pl.CostEstimate(
                flops=1 << 31, bytes_accessed=1 << 23, transcendentals=1 << 22
            ),
            name="grads",
        )(table, keys, values, *blocks, *all_stats, *extra_in)

    dkv_other, dq_before = grads_of(
        meta_other,
        k_other,
        v_other,
        False,
        [],
        [shape((half_rows, HEAD), BF16), shape((QSPANS * HEAD, COLS), F32)],
        [],
    )
    dkv_crossed = crossed(dkv_other)
    dkv_own, *dqs = grads_of(
        meta_own,
        k_own,
        v_own,
        True,
        [dq_before],
        [shape((half_rows, HEAD), BF16), shape((tokens, WIDTH), F32)]
        + [shape((tokens, WIDTH), BF16)] * (SHARE - 1),
        [pltpu.VMEM((tokens, WIDTH), F32), pltpu.VMEM((SHARE - 1, tokens, WIDTH), BF16)],
    )
    dkv_parts = exchanged((dkv_own.astype(F32) + dkv_crossed.astype(F32)).astype(BF16))
    dq_parts = [shifted(dqs[s], -s) for s in range(1, SHARE)]
    peers = (lax.axis_index("tp") + jnp.arange(tp_size, dtype=jnp.int32)) % tp_size
    feats = w_query.shape[0] // tp_size
    own, *pieces = pl.pallas_call(
        project_kernel,
        out_shape=[shape((tokens, feats), F32)] + [shape((tokens, feats), BF16)] * (tp_size - 1),
        in_specs=[SMEM] + [HBM] * 7 + [VMEM],
        out_specs=[VMEM] * tp_size,
        scratch_shapes=[
            pltpu.VMEM((tokens, WIDTH), F32),
            pltpu.VMEM((SHARE - 1, tokens, WIDTH), BF16),
            pltpu.VMEM((half_rows, HEAD), BF16),
            pltpu.VMEM(key_weight.shape, BF16),
            pltpu.VMEM(value_weight.shape, BF16),
            pltpu.SemaphoreType.DMA((7,)),
        ],
        compiler_params=SMALL,
        name="project",
    )(peers, dqs[0], *dq_parts, dkv_parts, key_weight, value_weight, w_query)
    for s in range(1, tp_size):
        pairs = [(d, (d + s) % tp_size) for d in range(tp_size)]
        own = own + lax.ppermute(pieces[s - 1], "tp", pairs).astype(F32)
    return own.astype(BF16)


def solution(mesh):
    row, col = P("ctx", "tp"), P(None, "tp")
    in_specs = (row, row, row, row, row, col, col, col, P())
    return jax.shard_map(local, mesh=mesh, in_specs=in_specs, out_specs=row, check_vma=False)
```

```python
import functools
import math

import jax
import jax.numpy as jnp
from jax import lax
from jax.experimental import pallas as pl
from jax.experimental.pallas import tpu as pltpu
from jax.sharding import PartitionSpec as P

HEAD = 128
SPAN = 64
GROUP = 4
SHARE = 4
SIDES = 2
SUBS = 4
BLOCK = SUBS * SPAN
COLS = GROUP * SPAN
WIDTH = GROUP * HEAD
QSPANS = 2 * SHARE
STATS = 3 * QSPANS
SCALE = HEAD ** (-0.5)
LOG2E = math.log2(math.e)
SCALE2 = SCALE * LOG2E
NEG = -1e30
F32 = jnp.float32
BF16 = jnp.bfloat16


def dot(left, right, left_dim, right_dim):
    return lax.dot_general(
        left, right, (((left_dim,), (right_dim,)), ((), ())), preferred_element_type=F32
    )


def rows_at(index, size):
    return pl.ds(pl.multiple_of(index * size, size), size)


def span_rows(slot, value):
    return rows_at(slot // 2 * 4 + slot % 2 + 2 * value, SPAN)


def load_all(sources, buffers, sems):
    copies = [
        pltpu.make_async_copy(source, buffer, sems.at[n])
        for n, (source, buffer) in enumerate(zip(sources, buffers))
    ]
    for copy in copies:
        copy.start()
    return copies


def head_cols(head, first=0):
    return slice(first + head * HEAD, first + (head + 1) * HEAD)


def span_slice(half):
    return slice(half * SPAN, (half + 1) * SPAN)


def part_slice(index, size):
    return slice(index * size, (index + 1) * size)


def pack_kernel(k_ref, v_ref, q_ref, g_ref, o_ref, copies_ref, out_ref, start_ref):
    tokens = k_ref.shape[0]
    for member in range(copies_ref.shape[0] // (2 * tokens)):
        copies_ref[part_slice(2 * member, tokens), :] = k_ref[...]
        copies_ref[part_slice(2 * member + 1, tokens), :] = v_ref[...]
    start_ref[:QSPANS, :] = jnp.full((QSPANS, COLS), NEG, F32)
    start_ref[QSPANS:, :] = jnp.zeros((STATS - QSPANS, COLS), F32)
    ones = jnp.ones((8, HEAD), BF16)
    for half in range(2):
        products = []
        for h in range(GROUP):
            rows, tokens = part_slice(half * GROUP + h, SPAN), span_slice(half)
            grad = g_ref[tokens, head_cols(h)]
            out_ref[rows, :HEAD] = q_ref[tokens, head_cols(h)]
            out_ref[rows, HEAD:] = grad
            products.append(grad.astype(F32) * o_ref[tokens, head_cols(h)].astype(F32))
        rest = jnp.concatenate(products, axis=0)
        delta = jnp.zeros((8, COLS), F32)
        for _ in range(3):
            part = rest.astype(BF16)
            delta = delta + dot(ones, part, 1, 1)
            rest = rest - part.astype(F32)
        start_ref[2 * QSPANS + half : 2 * QSPANS + half + 1, :] = delta[:1]


def mask_pattern():
    row = lax.broadcasted_iota(jnp.int32, (SPAN, COLS), 0)
    col = lax.broadcasted_iota(jnp.int32, (SPAN, COLS), 1)
    return row - col % SPAN


def slot_steps(meta, spans, steps, slot):
    count = steps // SHARE
    starts = [2 * spans + 3 * (slot * count + n) for n in range(count)]
    return [(meta[at], meta[at + 1], meta[at + 2]) for at in starts]


def slot_rows(ref, slot):
    return ref.at[part_slice(slot, 2 * COLS)]


def stats_kernel(spans, steps, meta, k_ref, b0, b1, b2, b3, before, out_ref, kin, ks, qs, ms, ls, sems):
    copies = load_all(
        (k_ref, *[b.at[:, :HEAD] for b in (b0, b1, b2, b3)]),
        (kin, *[slot_rows(qs, n) for n in range(SHARE)]),
        sems,
    )
    copies[0].wait()

    def copy_span(n, carry):
        ks[rows_at(n, SPAN), :] = kin[rows_at(meta[n], SPAN), :]
        return carry

    lax.fori_loop(0, spans, copy_span, 0, unroll=8)
    ms[...] = jnp.full_like(ms, NEG)
    ls[...] = jnp.zeros_like(ls)
    pattern = mask_pattern()
    for slot in range(SHARE):
        copies[1 + slot].wait()
        todo = slot_steps(meta, spans, steps, slot)
        scores = [
            dot(ks[rows_at(block, BLOCK), :], qs[rows_at(q_at, COLS), :], 1, 1)
            for q_at, block, _ in todo
        ]
        tops, totals = [], []
        for (_, block, query_pos), score in zip(todo, scores):
            parts = []
            for sub in range(SUBS):
                gap = (query_pos - meta[spans + block * SUBS + sub]) * SPAN
                part = jnp.where(pattern <= gap, score[part_slice(sub, SPAN)] * SCALE2, NEG)
                parts.append(part.reshape(SPAN // 8, 8, COLS))
            top = functools.reduce(jnp.maximum, [jnp.max(part, axis=0) for part in parts])
            tops.append(top)
            totals.append(sum(jnp.sum(jnp.exp2(part - top[None]), axis=0) for part in parts))
        for (q_at, _, _), top, total in zip(todo, tops, totals):
            rows = rows_at(q_at, 8)
            old = ms[rows, :]
            new = jnp.maximum(old, top)
            ls[rows, :] = ls[rows, :] * jnp.exp2(old - new) + total * jnp.exp2(top - new)
            ms[rows, :] = new
    out_ref[2 * QSPANS :, :] = before[2 * QSPANS :, :]
    for i in range(QSPANS):
        run_max, run_sum = ms[part_slice(i, 8), :], ls[part_slice(i, 8), :]
        old_max, old_sum = before[i : i + 1, :], before[QSPANS + i : QSPANS + i + 1, :]
        top = jnp.maximum(jnp.max(run_max, axis=0, keepdims=True), old_max)
        total = jnp.sum(run_sum * jnp.exp2(run_max - top), axis=0, keepdims=True)
        out_ref[i : i + 1, :] = top
        out_ref[QSPANS + i : QSPANS + i + 1, :] = total + old_sum * jnp.exp2(old_max - top)


def grads_kernel(spans, steps, last, *refs):
    meta, k_ref, v_ref = refs[:3]
    blocks, stats, refs = refs[3:7], refs[7:11], refs[11:]
    if last:
        dq_before, dkv_ref, *dq_refs = refs[: 2 + SHARE]
        kin, vin, dkv, own, others, ks, vs, kt, dka, dva, qs, gs, lt, dl, dqa, sems = refs[6:]
    else:
        dkv_ref, dq_ref, kin, vin, dkv, ks, vs, kt, dka, dva, qs, gs, lt, dl, dqa, sems = refs
    copies = load_all(
        (k_ref, v_ref, *[b.at[:, :HEAD] for b in blocks], *[b.at[:, HEAD:] for b in blocks]),
        (
            kin,
            vin,
            *[slot_rows(qs, n) for n in range(SHARE)],
            *[slot_rows(gs, n) for n in range(SHARE)],
        ),
        sems,
    )
    if last:
        before = [dq_before.at[part_slice(n, 2 * HEAD)] for n in range(SHARE)]
        targets = [dqa.at[part_slice(n, 2 * HEAD)] for n in range(SHARE)]
        copies += load_all(before, targets, sems.at[2 * SHARE + 2 :])
    else:
        dqa[...] = jnp.zeros_like(dqa)
    dka[...] = jnp.zeros_like(dka)
    dva[...] = jnp.zeros_like(dva)
    copies[0].wait()
    copies[1].wait()

    def copy_span(n, carry):
        rows = rows_at(n, SPAN)
        ks[rows, :] = kin[rows_at(meta[n], SPAN), :]
        vs[rows, :] = vin[rows_at(meta[n], SPAN), :]
        return carry

    lax.fori_loop(0, spans, copy_span, 0, unroll=8)
    for block in range(spans // SUBS):
        kt[part_slice(block, HEAD), :] = ks[part_slice(block, BLOCK), :].astype(F32).T.astype(BF16)
    pattern = mask_pattern()
    for i in range(QSPANS):
        slot, half = i // 2, i % 2
        delta = stats[slot][2 * QSPANS + half : 2 * QSPANS + half + 1, :]
        dl[part_slice(i, 8), :] = jnp.broadcast_to(delta, (8, COLS))
        tops, sums = [], []
        for shift in range(SHARE):
            row = ((slot - shift) % SHARE) * 2 + half
            tops.append(stats[shift][row : row + 1, :])
            sums.append(stats[shift][QSPANS + row : QSPANS + row + 1, :])
        top = functools.reduce(jnp.maximum, tops)
        total = sum(s * jnp.exp2(t - top) for s, t in zip(sums, tops))
        lt[part_slice(i, 8), :] = jnp.broadcast_to(top + jnp.log(total) * LOG2E, (8, COLS))
    stores = []
    for slot in range(SHARE):
        for copy in copies[2 + slot :: SHARE]:
            copy.wait()
        todo = slot_steps(meta, spans, steps, slot)
        key_rows = [rows_at(block, BLOCK) for _, block, _ in todo]
        query_rows = [rows_at(q_at, COLS) for q_at, _, _ in todo]
        scores, grad_probs = [], []
        for kr, qr in zip(key_rows, query_rows):
            scores.append(dot(ks[kr, :], qs[qr, :], 1, 1))
            grad_probs.append(dot(vs[kr, :], gs[qr, :], 1, 1))
        probs, grad_scores = [], []
        for u, (q_at, block, query_pos) in enumerate(todo):
            log_total, delta = lt[rows_at(q_at, 8), :][None], dl[rows_at(q_at, 8), :][None]
            low, low_grad = [], []
            for sub in range(SUBS):
                gap = (query_pos - meta[spans + block * SUBS + sub]) * SPAN
                rows = part_slice(sub, SPAN)
                part = scores[u][rows].reshape(SPAN // 8, 8, COLS) * SCALE2 - log_total
                part = jnp.where(pattern <= gap, jnp.exp2(part.reshape(SPAN, COLS)), 0.0)
                low.append(part.astype(BF16))
                change = grad_probs[u][rows].reshape(SPAN // 8, 8, COLS) - delta
                low_grad.append((part * change.reshape(SPAN, COLS)).astype(BF16))
            probs.append(jnp.concatenate(low, axis=0))
            grad_scores.append(jnp.concatenate(low_grad, axis=0))
        to_value, to_key, to_query = [], [], []
        for u, (_, block, _) in enumerate(todo):
            to_value.append(dot(probs[u], gs[query_rows[u], :], 1, 0))
            to_key.append(dot(grad_scores[u], qs[query_rows[u], :], 1, 0))
            to_query.append(dot(kt[rows_at(block, HEAD), :], grad_scores[u], 1, 0))
        for u, (q_at, _, _) in enumerate(todo):
            dva[key_rows[u], :] += to_value[u]
            dka[key_rows[u], :] += to_key[u]
            dqa[rows_at(q_at, HEAD), :] += to_query[u]
        store_sem = sems.at[3 * SHARE + 2 + slot]
        if last:
            out = own if slot == 0 else others.at[slot - 1]
            for half in range(2):
                full = dqa[part_slice(2 * slot + half, HEAD), :].T * SCALE
                for h in range(GROUP):
                    out[span_slice(half), head_cols(h)] = full[part_slice(h, SPAN)].astype(out.dtype)
            stores.append(pltpu.make_async_copy(out, dq_refs[slot], store_sem))
        else:
            rows = part_slice(slot, 2 * HEAD)
            stores.append(pltpu.make_async_copy(dqa.at[rows], dq_ref.at[rows], store_sem))
        stores[-1].start()

    def place_span(n, carry):
        rows = rows_at(n, SPAN)
        dest = spans - 2 - meta[n] + 2 * (meta[n] % 2)
        dkv[span_rows(dest, 0), :] = (dka[rows, :] * SCALE).astype(dkv.dtype)
        dkv[span_rows(dest, 1), :] = dva[rows, :].astype(dkv.dtype)
        return carry

    lax.fori_loop(0, spans, place_span, 0, unroll=8)
    stores.append(pltpu.make_async_copy(dkv, dkv_ref, sems.at[4 * SHARE + 2]))
    stores[-1].start()
    for store in stores:
        store.wait()


def project_kernel(
    peers, d0, d1, d2, d3, dkv_ref, wk_ref, wv_ref, wq_ref, o0, o1, o2, o3,
    own, others, dkv, wk, wv, sems,
):
    tokens, feats = o0.shape
    copies = load_all(
        (d0, d1, d2, d3, dkv_ref, wk_ref, wv_ref),
        (own, *[others.at[n] for n in range(SHARE - 1)], dkv, wk, wv),
        sems,
    )
    for copy in copies[:SHARE]:
        copy.wait()
    query = own[...]
    for n in range(SHARE - 1):
        query = query + others[n].astype(F32)
    query = query.astype(BF16)
    rows = [rows_at(peers[s], feats) for s in range(SHARE)]
    totals = [dot(query, wq_ref[at, :], 1, 1) for at in rows]
    copies[SHARE].wait()
    sums = jnp.zeros((2 * tokens, HEAD), F32)
    for member in range(dkv.shape[0] // (2 * tokens)):
        sums = sums + dkv[part_slice(member, 2 * tokens), :].astype(F32)
    sums = sums.astype(BF16)
    for copy in copies[SHARE + 1 :]:
        copy.wait()
    for at, total, out in zip(rows, totals, (o0, o1, o2, o3)):
        total = total + dot(sums[:tokens], wk[at, :], 1, 1)
        total = total + dot(sums[tokens:], wv[at, :], 1, 1)
        out[...] = total.astype(out.dtype)


VMEM = pl.BlockSpec(memory_space=pltpu.VMEM)
SMEM = pl.BlockSpec(memory_space=pltpu.SMEM)
HBM = pl.BlockSpec(memory_space=pltpu.HBM)
LARGE = pltpu.CompilerParams(vmem_limit_bytes=60 * 1024 * 1024)
SMALL = pltpu.CompilerParams(vmem_limit_bytes=16 * 1024 * 1024)


def shape(dims, dtype):
    return jax.ShapeDtypeStruct(dims, dtype)


def step_tables(span_pos, side, member, share, members, steps):
    spans = 2 * members
    cut = span_pos.reshape(SIDES, members, SHARE, 2)
    key_pos = lax.dynamic_slice_in_dim(cut, share, 1, axis=2).reshape(SIDES, spans)
    key_pos = jnp.where(side == 0, key_pos, key_pos[::-1])
    ids = jnp.arange(spans, dtype=jnp.int32)
    rank = jnp.sum((key_pos[:, None, :] < key_pos[:, :, None]).astype(jnp.int32), axis=2)
    placed = rank[:, None, :] == ids[None, :, None]
    order = jnp.sum(jnp.where(placed, ids[None, None, :], 0), axis=2)
    sorted_pos = jnp.sum(jnp.where(placed, key_pos[:, None, :], 0), axis=2)
    slots = jnp.arange(SHARE, dtype=jnp.int32)
    source = ((side * members + member) * SHARE + (share + SHARE - slots) % SHARE) * 2
    places = jnp.arange(span_pos.shape[0], dtype=jnp.int32)
    query_pos = [
        jnp.sum(jnp.where(places[None, :] == source[:, None] + h, span_pos[None, :], 0), axis=1)
        for h in range(2)
    ]
    blocks = [
        (jnp.sum((key_pos[:, None, :] <= qp[None, :, None]).astype(jnp.int32), axis=2) + SUBS - 1)
        // SUBS
        for qp in query_pos
    ]
    first, other = blocks[0][:, :, None], blocks[1][:, :, None]
    at = jnp.arange(steps // SHARE, dtype=jnp.int32)[None, None, :]
    second = at >= first
    block = jnp.where(second, at - first, at)
    used = jnp.logical_or(jnp.logical_not(second), block < other)
    q_at = jnp.where(second, 1, 0) + 2 * slots[None, :, None]
    pos = jnp.where(second, query_pos[1][None, :, None], query_pos[0][None, :, None])
    table = jnp.stack([q_at, jnp.where(used, block, 0), jnp.where(used, pos, -1)], axis=3)
    return jnp.concatenate([order, sorted_pos, table.reshape(SIDES, -1)], axis=1)


def local(q, k, v, o, g, w_query, key_weight, value_weight, span_pos):
    tokens = q.shape[0]
    cycle = lax.axis_size("ctx")
    tp_size = lax.axis_size("tp")
    members = cycle // SHARE // SIDES
    spans = 2 * members
    half_rows = 2 * spans * SPAN
    steps = SHARE * ((spans + 1 + 2 * (SUBS - 1)) // SUBS)
    index = lax.axis_index("ctx")
    share, member, side = index % SHARE, index // SHARE % members, index // (SHARE * members)

    def device(side_at, member_at, share_at):
        return (side_at % SIDES * members + member_at) * SHARE + share_at % SHARE

    places = [(a, b, c) for a in range(SIDES) for b in range(members) for c in range(SHARE)]
    key_groups = [
        [device(a, b, c) for b in range(members)] for a in range(SIDES) for c in range(SHARE)
    ]

    def exchanged(array, groups):
        return lax.all_to_all(array, "ctx", 0, 0, tiled=True, axis_index_groups=groups)

    def shifted(array, by):
        return lax.ppermute(array, "ctx", [(device(a, b, c), device(a, b, c + by)) for a, b, c in places])

    def crossed(array):
        return lax.ppermute(array, "ctx", [(device(a, b, c), device(a + 1, b, c)) for a, b, c in places])

    copies, block, start = pl.pallas_call(
        pack_kernel,
        out_shape=[
            shape((half_rows, HEAD), BF16),
            shape((2 * COLS, 2 * HEAD), BF16),
            shape((STATS, COLS), F32),
        ],
        in_specs=[VMEM] * 5,
        out_specs=[VMEM] * 3,
        name="pack",
    )(k, v, q, g, o)
    kv_own = exchanged(copies, key_groups)
    blocks = [block] + [shifted(block, s) for s in range(1, SHARE)]
    meta = step_tables(span_pos, side, member, share, members, steps)
    meta_own, meta_other = meta[0], meta[1]
    sides = kv_own.reshape(members, 2, tokens, HEAD)
    k_own, v_own = [sides[:, n].reshape(spans * SPAN, HEAD) for n in range(2)]
    k_other = crossed(k_own)

    def stats_of(table, keys, before):
        return pl.pallas_call(
            functools.partial(stats_kernel, spans, steps),
            out_shape=shape((STATS, COLS), F32),
            in_specs=[SMEM] + [HBM] * 5 + [VMEM],
            out_specs=VMEM,
            scratch_shapes=[
                pltpu.VMEM((spans * SPAN, HEAD), BF16),
                pltpu.VMEM((spans * SPAN, HEAD), BF16),
                pltpu.VMEM((QSPANS * COLS, HEAD), BF16),
                pltpu.VMEM((QSPANS * 8, COLS), F32),
                pltpu.VMEM((QSPANS * 8, COLS), F32),
                pltpu.SemaphoreType.DMA((5,)),
            ],
            compiler_params=LARGE,
            cost_estimate=pl.CostEstimate(
                flops=1 << 30, bytes_accessed=1 << 22, transcendentals=1 << 22
            ),
            name="stats",
        )(table, keys, *blocks, before)

    stats_own, v_late = lax.optimization_barrier((stats_of(meta_own, k_own, start), v_own))
    v_other = crossed(v_late)
    stats = stats_of(meta_other, k_other, stats_own)
    all_stats = [stats] + [shifted(stats, s) for s in range(1, SHARE)]

    def grads_of(table, keys, values, last, extra_in, outs, extra_scratch):
        return pl.pallas_call(
            functools.partial(grads_kernel, spans, steps, last),
            out_shape=outs,
            in_specs=[SMEM] + [HBM] * 6 + [VMEM] * 4 + [HBM] * len(extra_in),
            out_specs=[HBM] * len(outs),
            scratch_shapes=[
                pltpu.VMEM((spans * SPAN, HEAD), BF16),
                pltpu.VMEM((spans * SPAN, HEAD), BF16),
                pltpu.VMEM((half_rows, HEAD), outs[0].dtype),
                *extra_scratch,
                pltpu.VMEM((spans * SPAN, HEAD), BF16),
                pltpu.VMEM((spans * SPAN, HEAD), BF16),
                pltpu.VMEM((spans // SUBS * HEAD, BLOCK), BF16),
                pltpu.VMEM((spans * SPAN, HEAD), F32),
                pltpu.VMEM((spans * SPAN, HEAD), F32),
                pltpu.VMEM((QSPANS * COLS, HEAD), BF16),
                pltpu.VMEM((QSPANS * COLS, HEAD), BF16),
                pltpu.VMEM((QSPANS * 8, COLS), F32),
                pltpu.VMEM((QSPANS * 8, COLS), F32),
                pltpu.VMEM((QSPANS * HEAD, COLS), F32),
                pltpu.SemaphoreType.DMA((4 * SHARE + 3,)),
            ],
            compiler_params=LARGE,
            cost_estimate=pl.CostEstimate(
                flops=1 << 31, bytes_accessed=1 << 23, transcendentals=1 << 22
            ),
            name="grads",
        )(table, keys, values, *blocks, *all_stats, *extra_in)

    dkv_other, dq_before = grads_of(
        meta_other,
        k_other,
        v_other,
        False,
        [],
        [shape((half_rows, HEAD), BF16), shape((QSPANS * HEAD, COLS), F32)],
        [],
    )
    dkv_crossed = crossed(dkv_other)
    dkv_own, *dqs = grads_of(
        meta_own,
        k_own,
        v_own,
        True,
        [dq_before],
        [shape((half_rows, HEAD), BF16), shape((tokens, WIDTH), F32)]
        + [shape((tokens, WIDTH), BF16)] * (SHARE - 1),
        [pltpu.VMEM((tokens, WIDTH), F32), pltpu.VMEM((SHARE - 1, tokens, WIDTH), BF16)],
    )
    turned_groups = [group[::-1] for group in key_groups]
    dkv_parts = exchanged((dkv_own.astype(F32) + dkv_crossed.astype(F32)).astype(BF16), turned_groups)
    dq_parts = [shifted(dqs[s], -s) for s in range(1, SHARE)]
    peers = (lax.axis_index("tp") + jnp.arange(tp_size, dtype=jnp.int32)) % tp_size
    feats = w_query.shape[0] // tp_size
    own, *pieces = pl.pallas_call(
        project_kernel,
        out_shape=[shape((tokens, feats), F32)] + [shape((tokens, feats), BF16)] * (tp_size - 1),
        in_specs=[SMEM] + [HBM] * 7 + [VMEM],
        out_specs=[VMEM] * tp_size,
        scratch_shapes=[
            pltpu.VMEM((tokens, WIDTH), F32),
            pltpu.VMEM((SHARE - 1, tokens, WIDTH), BF16),
            pltpu.VMEM((half_rows, HEAD), BF16),
            pltpu.VMEM(key_weight.shape, BF16),
            pltpu.VMEM(value_weight.shape, BF16),
            pltpu.SemaphoreType.DMA((7,)),
        ],
        compiler_params=SMALL,
        name="project",
    )(peers, dqs[0], *dq_parts, dkv_parts, key_weight, value_weight, w_query)
    for s in range(1, tp_size):
        pairs = [(d, (d + s) % tp_size) for d in range(tp_size)]
        own = own + lax.ppermute(pieces[s - 1], "tp", pairs).astype(F32)
    return own.astype(BF16)


def solution(mesh):
    row, col = P("ctx", "tp"), P(None, "tp")
    in_specs = (row, row, row, row, row, col, col, col, P())
    return jax.shard_map(local, mesh=mesh, in_specs=in_specs, out_specs=row, check_vma=False)
```

```python
import functools
import math

import jax
import jax.numpy as jnp
from jax import lax
from jax.experimental import pallas as pl
from jax.experimental.pallas import tpu as pltpu
from jax.sharding import PartitionSpec as P

HEAD = 128
SPAN = 64
GROUP = 4
SHARE = 4
SIDES = 2
SUBS = 4
BLOCK = SUBS * SPAN
COLS = GROUP * SPAN
WIDTH = GROUP * HEAD
QSPANS = 2 * SHARE
STATS = 3 * QSPANS
SCALE = HEAD ** (-0.5)
LOG2E = math.log2(math.e)
SCALE2 = SCALE * LOG2E
NEG = -1e30
F32 = jnp.float32
BF16 = jnp.bfloat16


def dot(left, right, left_dim, right_dim):
    return lax.dot_general(
        left, right, (((left_dim,), (right_dim,)), ((), ())), preferred_element_type=F32
    )


def rows_at(index, size):
    return pl.ds(pl.multiple_of(index * size, size), size)


def span_rows(slot, value):
    return rows_at(slot // 2 * 4 + slot % 2 + 2 * value, SPAN)


def load_all(sources, buffers, sems):
    copies = [
        pltpu.make_async_copy(source, buffer, sems.at[n])
        for n, (source, buffer) in enumerate(zip(sources, buffers))
    ]
    for copy in copies:
        copy.start()
    return copies


def head_cols(head, first=0):
    return slice(first + head * HEAD, first + (head + 1) * HEAD)


def span_slice(half):
    return slice(half * SPAN, (half + 1) * SPAN)


def part_slice(index, size):
    return slice(index * size, (index + 1) * size)


def pack_kernel(k_ref, v_ref, q_ref, g_ref, o_ref, copies_ref, out_ref, start_ref):
    tokens = k_ref.shape[0]
    for member in range(copies_ref.shape[0] // (2 * tokens)):
        copies_ref[part_slice(2 * member, tokens), :] = k_ref[...]
        copies_ref[part_slice(2 * member + 1, tokens), :] = v_ref[...]
    start_ref[:QSPANS, :] = jnp.full((QSPANS, COLS), NEG, F32)
    start_ref[QSPANS:, :] = jnp.zeros((STATS - QSPANS, COLS), F32)
    ones = jnp.ones((8, HEAD), BF16)
    for half in range(2):
        products = []
        for h in range(GROUP):
            rows, tokens = part_slice(half * GROUP + h, SPAN), span_slice(half)
            grad = g_ref[tokens, head_cols(h)]
            out_ref[rows, :HEAD] = q_ref[tokens, head_cols(h)]
            out_ref[rows, HEAD:] = grad
            products.append(grad.astype(F32) * o_ref[tokens, head_cols(h)].astype(F32))
        rest = jnp.concatenate(products, axis=0)
        delta = jnp.zeros((8, COLS), F32)
        for _ in range(3):
            part = rest.astype(BF16)
            delta = delta + dot(ones, part, 1, 1)
            rest = rest - part.astype(F32)
        start_ref[2 * QSPANS + half : 2 * QSPANS + half + 1, :] = delta[:1]


def mask_pattern():
    row = lax.broadcasted_iota(jnp.int32, (SPAN, COLS), 0)
    col = lax.broadcasted_iota(jnp.int32, (SPAN, COLS), 1)
    return row - col % SPAN


def slot_steps(meta, spans, steps, slot):
    count = steps // SHARE
    starts = [2 * spans + 3 * (slot * count + n) for n in range(count)]
    return [(meta[at], meta[at + 1], meta[at + 2]) for at in starts]


def slot_rows(ref, slot):
    return ref.at[part_slice(slot, 2 * COLS)]


def stats_kernel(spans, steps, meta, k_ref, b0, b1, b2, b3, before, *refs):
    moves = []
    if len(refs) == 11:
        weights, out_ref, joined, held = refs[:2], refs[2], refs[3], refs[4]
        halves = [held.at[part_slice(n, joined.shape[0] // 2)] for n in range(2)]
        kin, ks, qs, ms, ls, sems = refs[5:]
    else:
        weights, halves, out_ref, (kin, ks, qs, ms, ls, sems) = [], [], refs[0], refs[1:]
    copies = load_all(
        (k_ref, *[b.at[:, :HEAD] for b in (b0, b1, b2, b3)]),
        (kin, *[slot_rows(qs, n) for n in range(SHARE)]),
        sems,
    )
    fetched = load_all(weights, halves, sems.at[SHARE + 1 :])
    copies[0].wait()

    def copy_span(n, carry):
        ks[rows_at(n, SPAN), :] = kin[rows_at(meta[n], SPAN), :]
        return carry

    lax.fori_loop(0, spans, copy_span, 0, unroll=8)
    ms[...] = jnp.full_like(ms, NEG)
    ls[...] = jnp.zeros_like(ls)
    pattern = mask_pattern()
    for slot in range(SHARE):
        if slot == 1 and fetched:
            for copy in fetched:
                copy.wait()
            moves.append(pltpu.make_async_copy(held, joined, sems.at[SHARE + 3]))
            moves[0].start()
        copies[1 + slot].wait()
        todo = slot_steps(meta, spans, steps, slot)
        scores = [
            dot(ks[rows_at(block, BLOCK), :], qs[rows_at(q_at, COLS), :], 1, 1)
            for q_at, block, _ in todo
        ]
        tops, totals = [], []
        for (_, block, query_pos), score in zip(todo, scores):
            parts = []
            for sub in range(SUBS):
                gap = (query_pos - meta[spans + block * SUBS + sub]) * SPAN
                part = jnp.where(pattern <= gap, score[part_slice(sub, SPAN)] * SCALE2, NEG)
                parts.append(part.reshape(SPAN // 8, 8, COLS))
            top = functools.reduce(jnp.maximum, [jnp.max(part, axis=0) for part in parts])
            tops.append(top)
            totals.append(sum(jnp.sum(jnp.exp2(part - top[None]), axis=0) for part in parts))
        for (q_at, _, _), top, total in zip(todo, tops, totals):
            rows = rows_at(q_at, 8)
            old = ms[rows, :]
            new = jnp.maximum(old, top)
            ls[rows, :] = ls[rows, :] * jnp.exp2(old - new) + total * jnp.exp2(top - new)
            ms[rows, :] = new
    out_ref[2 * QSPANS :, :] = before[2 * QSPANS :, :]
    for i in range(QSPANS):
        run_max, run_sum = ms[part_slice(i, 8), :], ls[part_slice(i, 8), :]
        old_max, old_sum = before[i : i + 1, :], before[QSPANS + i : QSPANS + i + 1, :]
        top = jnp.maximum(jnp.max(run_max, axis=0, keepdims=True), old_max)
        total = jnp.sum(run_sum * jnp.exp2(run_max - top), axis=0, keepdims=True)
        out_ref[i : i + 1, :] = top
        out_ref[QSPANS + i : QSPANS + i + 1, :] = total + old_sum * jnp.exp2(old_max - top)
    for move in moves:
        move.wait()


def grads_kernel(spans, steps, last, *refs):
    meta, k_ref, v_ref = refs[:3]
    blocks, stats, refs = refs[3:7], refs[7:11], refs[11:]
    if last:
        dq_before, dkv_ref, *dq_refs = refs[: 2 + SHARE]
        kin, vin, dkv, own, others, ks, vs, kt, dka, dva, qs, gs, lt, dl, dqa, sems = refs[6:]
    else:
        dkv_ref, dq_ref, kin, vin, dkv, ks, vs, kt, dka, dva, qs, gs, lt, dl, dqa, sems = refs
    copies = load_all(
        (k_ref, v_ref, *[b.at[:, :HEAD] for b in blocks], *[b.at[:, HEAD:] for b in blocks]),
        (
            kin,
            vin,
            *[slot_rows(qs, n) for n in range(SHARE)],
            *[slot_rows(gs, n) for n in range(SHARE)],
        ),
        sems,
    )
    if last:
        before = [dq_before.at[part_slice(n, 2 * HEAD)] for n in range(SHARE)]
        targets = [dqa.at[part_slice(n, 2 * HEAD)] for n in range(SHARE)]
        copies += load_all(before, targets, sems.at[2 * SHARE + 2 :])
    else:
        dqa[...] = jnp.zeros_like(dqa)
    dka[...] = jnp.zeros_like(dka)
    dva[...] = jnp.zeros_like(dva)
    copies[0].wait()
    copies[1].wait()

    def copy_span(n, carry):
        rows = rows_at(n, SPAN)
        ks[rows, :] = kin[rows_at(meta[n], SPAN), :]
        vs[rows, :] = vin[rows_at(meta[n], SPAN), :]
        return carry

    lax.fori_loop(0, spans, copy_span, 0, unroll=8)
    for block in range(spans // SUBS):
        kt[part_slice(block, HEAD), :] = ks[part_slice(block, BLOCK), :].astype(F32).T.astype(BF16)
    pattern = mask_pattern()
    for i in range(QSPANS):
        slot, half = i // 2, i % 2
        delta = stats[slot][2 * QSPANS + half : 2 * QSPANS + half + 1, :]
        dl[part_slice(i, 8), :] = jnp.broadcast_to(delta, (8, COLS))
        tops, sums = [], []
        for shift in range(SHARE):
            row = ((slot - shift) % SHARE) * 2 + half
            tops.append(stats[shift][row : row + 1, :])
            sums.append(stats[shift][QSPANS + row : QSPANS + row + 1, :])
        top = functools.reduce(jnp.maximum, tops)
        total = sum(s * jnp.exp2(t - top) for s, t in zip(sums, tops))
        lt[part_slice(i, 8), :] = jnp.broadcast_to(top + jnp.log(total) * LOG2E, (8, COLS))
    stores = []
    for slot in range(SHARE):
        for copy in copies[2 + slot :: SHARE]:
            copy.wait()
        todo = slot_steps(meta, spans, steps, slot)
        key_rows = [rows_at(block, BLOCK) for _, block, _ in todo]
        query_rows = [rows_at(q_at, COLS) for q_at, _, _ in todo]
        scores, grad_probs = [], []
        for kr, qr in zip(key_rows, query_rows):
            scores.append(dot(ks[kr, :], qs[qr, :], 1, 1))
            grad_probs.append(dot(vs[kr, :], gs[qr, :], 1, 1))
        probs, grad_scores = [], []
        for u, (q_at, block, query_pos) in enumerate(todo):
            log_total, delta = lt[rows_at(q_at, 8), :][None], dl[rows_at(q_at, 8), :][None]
            low, low_grad = [], []
            for sub in range(SUBS):
                gap = (query_pos - meta[spans + block * SUBS + sub]) * SPAN
                rows = part_slice(sub, SPAN)
                part = scores[u][rows].reshape(SPAN // 8, 8, COLS) * SCALE2 - log_total
                part = jnp.where(pattern <= gap, jnp.exp2(part.reshape(SPAN, COLS)), 0.0)
                low.append(part.astype(BF16))
                change = grad_probs[u][rows].reshape(SPAN // 8, 8, COLS) - delta
                low_grad.append((part * change.reshape(SPAN, COLS)).astype(BF16))
            probs.append(jnp.concatenate(low, axis=0))
            grad_scores.append(jnp.concatenate(low_grad, axis=0))
        to_value, to_key, to_query = [], [], []
        for u, (_, block, _) in enumerate(todo):
            to_value.append(dot(probs[u], gs[query_rows[u], :], 1, 0))
            to_key.append(dot(grad_scores[u], qs[query_rows[u], :], 1, 0))
            to_query.append(dot(kt[rows_at(block, HEAD), :], grad_scores[u], 1, 0))
        for u, (q_at, _, _) in enumerate(todo):
            dva[key_rows[u], :] += to_value[u]
            dka[key_rows[u], :] += to_key[u]
            dqa[rows_at(q_at, HEAD), :] += to_query[u]
        store_sem = sems.at[3 * SHARE + 2 + slot]
        if last:
            out = own if slot == 0 else others.at[slot - 1]
            for half in range(2):
                full = dqa[part_slice(2 * slot + half, HEAD), :].T * SCALE
                for h in range(GROUP):
                    out[span_slice(half), head_cols(h)] = full[part_slice(h, SPAN)].astype(out.dtype)
            stores.append(pltpu.make_async_copy(out, dq_refs[slot], store_sem))
        else:
            rows = part_slice(slot, 2 * HEAD)
            stores.append(pltpu.make_async_copy(dqa.at[rows], dq_ref.at[rows], store_sem))
        stores[-1].start()

    def place_span(n, carry):
        rows = rows_at(n, SPAN)
        dest = spans - 2 - meta[n] + 2 * (meta[n] % 2)
        dkv[span_rows(dest, 0), :] = (dka[rows, :] * SCALE).astype(dkv.dtype)
        dkv[span_rows(dest, 1), :] = dva[rows, :].astype(dkv.dtype)
        return carry

    lax.fori_loop(0, spans, place_span, 0, unroll=8)
    stores.append(pltpu.make_async_copy(dkv, dkv_ref, sems.at[4 * SHARE + 2]))
    stores[-1].start()
    for store in stores:
        store.wait()


def project_kernel(
    peers, d0, d1, d2, d3, dkv_ref, narrow_ref, wq_ref, o0, o1, o2, o3,
    own, others, dkv, narrow, sems,
):
    tokens, feats = o0.shape
    copies = load_all(
        (d0, d1, d2, d3, dkv_ref, narrow_ref),
        (own, *[others.at[n] for n in range(SHARE - 1)], dkv, narrow),
        sems,
    )
    for copy in copies[:SHARE]:
        copy.wait()
    query = own[...]
    for n in range(SHARE - 1):
        query = query + others[n].astype(F32)
    query = query.astype(BF16)
    rows = [rows_at(peers[s], feats) for s in range(SHARE)]
    totals = [dot(query, wq_ref[at, :], 1, 1) for at in rows]
    copies[SHARE].wait()
    sums = jnp.zeros((2 * tokens, HEAD), F32)
    for member in range(dkv.shape[0] // (2 * tokens)):
        sums = sums + dkv[part_slice(member, 2 * tokens), :].astype(F32)
    sums = sums.astype(BF16)
    for copy in copies[SHARE + 1 :]:
        copy.wait()
    lower = [rows_at(peers[s] + SHARE, feats) for s in range(SHARE)]
    for at, low, total, out in zip(rows, lower, totals, (o0, o1, o2, o3)):
        total = total + dot(sums[:tokens], narrow[at, :], 1, 1)
        total = total + dot(sums[tokens:], narrow[low, :], 1, 1)
        out[...] = total.astype(out.dtype)


VMEM = pl.BlockSpec(memory_space=pltpu.VMEM)
SMEM = pl.BlockSpec(memory_space=pltpu.SMEM)
HBM = pl.BlockSpec(memory_space=pltpu.HBM)
LARGE = pltpu.CompilerParams(vmem_limit_bytes=60 * 1024 * 1024)
SMALL = pltpu.CompilerParams(vmem_limit_bytes=16 * 1024 * 1024)


def shape(dims, dtype):
    return jax.ShapeDtypeStruct(dims, dtype)


def step_tables(span_pos, side, member, share, members, steps):
    spans = 2 * members
    cut = span_pos.reshape(SIDES, members, SHARE, 2)
    key_pos = lax.dynamic_slice_in_dim(cut, share, 1, axis=2).reshape(SIDES, spans)
    key_pos = jnp.where(side == 0, key_pos, key_pos[::-1])
    ids = jnp.arange(spans, dtype=jnp.int32)
    rank = jnp.sum((key_pos[:, None, :] < key_pos[:, :, None]).astype(jnp.int32), axis=2)
    placed = rank[:, None, :] == ids[None, :, None]
    order = jnp.sum(jnp.where(placed, ids[None, None, :], 0), axis=2)
    sorted_pos = jnp.sum(jnp.where(placed, key_pos[:, None, :], 0), axis=2)
    slots = jnp.arange(SHARE, dtype=jnp.int32)
    source = ((side * members + member) * SHARE + (share + SHARE - slots) % SHARE) * 2
    places = jnp.arange(span_pos.shape[0], dtype=jnp.int32)
    query_pos = [
        jnp.sum(jnp.where(places[None, :] == source[:, None] + h, span_pos[None, :], 0), axis=1)
        for h in range(2)
    ]
    blocks = [
        (jnp.sum((key_pos[:, None, :] <= qp[None, :, None]).astype(jnp.int32), axis=2) + SUBS - 1)
        // SUBS
        for qp in query_pos
    ]
    first, other = blocks[0][:, :, None], blocks[1][:, :, None]
    at = jnp.arange(steps // SHARE, dtype=jnp.int32)[None, None, :]
    second = at >= first
    block = jnp.where(second, at - first, at)
    used = jnp.logical_or(jnp.logical_not(second), block < other)
    q_at = jnp.where(second, 1, 0) + 2 * slots[None, :, None]
    pos = jnp.where(second, query_pos[1][None, :, None], query_pos[0][None, :, None])
    table = jnp.stack([q_at, jnp.where(used, block, 0), jnp.where(used, pos, -1)], axis=3)
    return jnp.concatenate([order, sorted_pos, table.reshape(SIDES, -1)], axis=1)


def local(q, k, v, o, g, w_query, key_weight, value_weight, span_pos):
    tokens = q.shape[0]
    cycle = lax.axis_size("ctx")
    tp_size = lax.axis_size("tp")
    members = cycle // SHARE // SIDES
    spans = 2 * members
    half_rows = 2 * spans * SPAN
    steps = SHARE * ((spans + 1 + 2 * (SUBS - 1)) // SUBS)
    index = lax.axis_index("ctx")
    share, member, side = index % SHARE, index // SHARE % members, index // (SHARE * members)

    def device(side_at, member_at, share_at):
        return (side_at % SIDES * members + member_at) * SHARE + share_at % SHARE

    places = [(a, b, c) for a in range(SIDES) for b in range(members) for c in range(SHARE)]
    key_groups = [
        [device(a, b, c) for b in range(members)] for a in range(SIDES) for c in range(SHARE)
    ]

    def exchanged(array, groups):
        return lax.all_to_all(array, "ctx", 0, 0, tiled=True, axis_index_groups=groups)

    def shifted(array, by):
        return lax.ppermute(array, "ctx", [(device(a, b, c), device(a, b, c + by)) for a, b, c in places])

    def crossed(array):
        return lax.ppermute(array, "ctx", [(device(a, b, c), device(a + 1, b, c)) for a, b, c in places])

    copies, block, start = pl.pallas_call(
        pack_kernel,
        out_shape=[
            shape((half_rows, HEAD), BF16),
            shape((2 * COLS, 2 * HEAD), BF16),
            shape((STATS, COLS), F32),
        ],
        in_specs=[VMEM] * 5,
        out_specs=[VMEM] * 3,
        name="pack",
    )(k, v, q, g, o)
    kv_own = exchanged(copies, key_groups)
    blocks = [block] + [shifted(block, s) for s in range(1, SHARE)]
    meta = step_tables(span_pos, side, member, share, members, steps)
    meta_own, meta_other = meta[0], meta[1]
    sides = kv_own.reshape(members, 2, tokens, HEAD)
    k_own, v_own = [sides[:, n].reshape(spans * SPAN, HEAD) for n in range(2)]
    k_other = crossed(k_own)

    def stats_of(table, keys, before, weights):
        return pl.pallas_call(
            functools.partial(stats_kernel, spans, steps),
            out_shape=[shape((STATS, COLS), F32)]
            + [shape((2 * w.shape[0], HEAD), BF16) for w in weights[:1]],
            in_specs=[SMEM] + [HBM] * 5 + [VMEM] + [HBM] * len(weights),
            out_specs=[VMEM] + [HBM] * len(weights[:1]),
            scratch_shapes=[
                *[pltpu.VMEM((2 * w.shape[0], HEAD), BF16) for w in weights[:1]],
                pltpu.VMEM((spans * SPAN, HEAD), BF16),
                pltpu.VMEM((spans * SPAN, HEAD), BF16),
                pltpu.VMEM((QSPANS * COLS, HEAD), BF16),
                pltpu.VMEM((QSPANS * 8, COLS), F32),
                pltpu.VMEM((QSPANS * 8, COLS), F32),
                pltpu.SemaphoreType.DMA((8,)),
            ],
            compiler_params=LARGE,
            cost_estimate=pl.CostEstimate(
                flops=1 << 30, bytes_accessed=1 << 22, transcendentals=1 << 22
            ),
            name="stats",
        )(table, keys, *blocks, before, *weights)

    stats_own, narrow = stats_of(meta_own, k_own, start, [key_weight, value_weight])
    stats_own, v_late = lax.optimization_barrier((stats_own, v_own))
    v_other = crossed(v_late)
    (stats,) = stats_of(meta_other, k_other, stats_own, [])
    all_stats = [stats] + [shifted(stats, s) for s in range(1, SHARE)]

    def grads_of(table, keys, values, last, extra_in, outs, extra_scratch):
        return pl.pallas_call(
            functools.partial(grads_kernel, spans, steps, last),
            out_shape=outs,
            in_specs=[SMEM] + [HBM] * 6 + [VMEM] * 4 + [HBM] * len(extra_in),
            out_specs=[HBM] * len(outs),
            scratch_shapes=[
                pltpu.VMEM((spans * SPAN, HEAD), BF16),
                pltpu.VMEM((spans * SPAN, HEAD), BF16),
                pltpu.VMEM((half_rows, HEAD), outs[0].dtype),
                *extra_scratch,
                pltpu.VMEM((spans * SPAN, HEAD), BF16),
                pltpu.VMEM((spans * SPAN, HEAD), BF16),
                pltpu.VMEM((spans // SUBS * HEAD, BLOCK), BF16),
                pltpu.VMEM((spans * SPAN, HEAD), F32),
                pltpu.VMEM((spans * SPAN, HEAD), F32),
                pltpu.VMEM((QSPANS * COLS, HEAD), BF16),
                pltpu.VMEM((QSPANS * COLS, HEAD), BF16),
                pltpu.VMEM((QSPANS * 8, COLS), F32),
                pltpu.VMEM((QSPANS * 8, COLS), F32),
                pltpu.VMEM((QSPANS * HEAD, COLS), F32),
                pltpu.SemaphoreType.DMA((4 * SHARE + 3,)),
            ],
            compiler_params=LARGE,
            cost_estimate=pl.CostEstimate(
                flops=1 << 31, bytes_accessed=1 << 23, transcendentals=1 << 22
            ),
            name="grads",
        )(table, keys, values, *blocks, *all_stats, *extra_in)

    dkv_other, dq_before = grads_of(
        meta_other,
        k_other,
        v_other,
        False,
        [],
        [shape((half_rows, HEAD), BF16), shape((QSPANS * HEAD, COLS), F32)],
        [],
    )
    dkv_crossed = crossed(dkv_other)
    dkv_own, *dqs = grads_of(
        meta_own,
        k_own,
        v_own,
        True,
        [dq_before],
        [shape((half_rows, HEAD), BF16), shape((tokens, WIDTH), F32)]
        + [shape((tokens, WIDTH), BF16)] * (SHARE - 1),
        [pltpu.VMEM((tokens, WIDTH), F32), pltpu.VMEM((SHARE - 1, tokens, WIDTH), BF16)],
    )
    turned_groups = [group[::-1] for group in key_groups]
    dkv_parts = exchanged((dkv_own.astype(F32) + dkv_crossed.astype(F32)).astype(BF16), turned_groups)
    dq_parts = [shifted(dqs[s], -s) for s in range(1, SHARE)]
    peers = (lax.axis_index("tp") + jnp.arange(tp_size, dtype=jnp.int32)) % tp_size
    feats = w_query.shape[0] // tp_size
    own, *pieces = pl.pallas_call(
        project_kernel,
        out_shape=[shape((tokens, feats), F32)] + [shape((tokens, feats), BF16)] * (tp_size - 1),
        in_specs=[SMEM] + [HBM] * 6 + [VMEM],
        out_specs=[VMEM] * tp_size,
        scratch_shapes=[
            pltpu.VMEM((tokens, WIDTH), F32),
            pltpu.VMEM((SHARE - 1, tokens, WIDTH), BF16),
            pltpu.VMEM((half_rows, HEAD), BF16),
            pltpu.VMEM(narrow.shape, BF16),
            pltpu.SemaphoreType.DMA((6,)),
        ],
        compiler_params=SMALL,
        name="project",
    )(peers, dqs[0], *dq_parts, dkv_parts, narrow, w_query)
    for s in range(1, tp_size):
        pairs = [(d, (d + s) % tp_size) for d in range(tp_size)]
        own = own + lax.ppermute(pieces[s - 1], "tp", pairs).astype(F32)
    return own.astype(BF16)


def solution(mesh):
    row, col = P("ctx", "tp"), P(None, "tp")
    in_specs = (row, row, row, row, row, col, col, col, P())
    return jax.shard_map(local, mesh=mesh, in_specs=in_specs, out_specs=row, check_vma=False)
```

```python
import functools
import math

import jax
import jax.numpy as jnp
from jax import lax
from jax.experimental import pallas as pl
from jax.experimental.pallas import tpu as pltpu
from jax.sharding import PartitionSpec as P

HEAD = 128
SPAN = 64
GROUP = 4
SHARE = 4
SIDES = 2
SUBS = 4
BLOCK = SUBS * SPAN
COLS = GROUP * SPAN
WIDTH = GROUP * HEAD
QSPANS = 2 * SHARE
STATS = 3 * QSPANS
SCALE = HEAD ** (-0.5)
LOG2E = math.log2(math.e)
SCALE2 = SCALE * LOG2E
NEG = -1e30
F32 = jnp.float32
BF16 = jnp.bfloat16


def dot(left, right, left_dim, right_dim):
    return lax.dot_general(
        left, right, (((left_dim,), (right_dim,)), ((), ())), preferred_element_type=F32
    )


def rows_at(index, size):
    return pl.ds(pl.multiple_of(index * size, size), size)


def span_rows(slot, value):
    return rows_at(slot // 2 * 4 + slot % 2 + 2 * value, SPAN)


def load_all(sources, buffers, sems):
    copies = [
        pltpu.make_async_copy(source, buffer, sems.at[n])
        for n, (source, buffer) in enumerate(zip(sources, buffers))
    ]
    for copy in copies:
        copy.start()
    return copies


def head_cols(head, first=0):
    return slice(first + head * HEAD, first + (head + 1) * HEAD)


def span_slice(half):
    return slice(half * SPAN, (half + 1) * SPAN)


def part_slice(index, size):
    return slice(index * size, (index + 1) * size)


def pack_kernel(k_ref, v_ref, q_ref, g_ref, o_ref, copies_ref, out_ref, start_ref):
    tokens = k_ref.shape[0]
    for member in range(copies_ref.shape[0] // (2 * tokens)):
        copies_ref[part_slice(2 * member, tokens), :] = k_ref[...]
        copies_ref[part_slice(2 * member + 1, tokens), :] = v_ref[...]
    start_ref[:QSPANS, :] = jnp.full((QSPANS, COLS), NEG, F32)
    start_ref[QSPANS:, :] = jnp.zeros((STATS - QSPANS, COLS), F32)
    ones = jnp.ones((8, HEAD), BF16)
    for half in range(2):
        products = []
        for h in range(GROUP):
            rows, tokens = part_slice(half * GROUP + h, SPAN), span_slice(half)
            grad = g_ref[tokens, head_cols(h)]
            out_ref[rows, :HEAD] = q_ref[tokens, head_cols(h)]
            out_ref[rows, HEAD:] = grad
            products.append(grad.astype(F32) * o_ref[tokens, head_cols(h)].astype(F32))
        rest = jnp.concatenate(products, axis=0)
        delta = jnp.zeros((8, COLS), F32)
        for _ in range(3):
            part = rest.astype(BF16)
            delta = delta + dot(ones, part, 1, 1)
            rest = rest - part.astype(F32)
        start_ref[2 * QSPANS + half : 2 * QSPANS + half + 1, :] = delta[:1]


def mask_pattern():
    row = lax.broadcasted_iota(jnp.int32, (SPAN, COLS), 0)
    col = lax.broadcasted_iota(jnp.int32, (SPAN, COLS), 1)
    return row - col % SPAN


def slot_steps(meta, spans, steps, slot):
    count = steps // SHARE
    starts = [2 * spans + 3 * (slot * count + n) for n in range(count)]
    return [(meta[at], meta[at + 1], meta[at + 2]) for at in starts]


def slot_rows(ref, slot):
    return ref.at[part_slice(slot, 2 * COLS)]


def stats_kernel(spans, steps, meta, k_ref, b0, b1, b2, b3, before, *refs):
    moves = []
    if len(refs) == 11:
        weights, out_ref, joined, held = refs[:2], refs[2], refs[3], refs[4]
        halves = [held.at[part_slice(n, joined.shape[0] // 2)] for n in range(2)]
        kin, ks, qs, ms, ls, sems = refs[5:]
    else:
        weights, halves, out_ref, (kin, ks, qs, ms, ls, sems) = [], [], refs[0], refs[1:]
    copies = load_all(
        (k_ref, *[b.at[:, :HEAD] for b in (b0, b1, b2, b3)]),
        (kin, *[slot_rows(qs, n) for n in range(SHARE)]),
        sems,
    )
    fetched = load_all(weights, halves, sems.at[SHARE + 1 :])
    copies[0].wait()

    def copy_span(n, carry):
        ks[rows_at(n, SPAN), :] = kin[rows_at(meta[n], SPAN), :]
        return carry

    lax.fori_loop(0, spans, copy_span, 0, unroll=8)
    ms[...] = jnp.full_like(ms, NEG)
    ls[...] = jnp.zeros_like(ls)
    pattern = mask_pattern()
    for slot in range(SHARE):
        if slot == 1 and fetched:
            for copy in fetched:
                copy.wait()
            moves.append(pltpu.make_async_copy(held, joined, sems.at[SHARE + 3]))
            moves[0].start()
        copies[1 + slot].wait()
        todo = slot_steps(meta, spans, steps, slot)
        scores = [
            dot(ks[rows_at(block, BLOCK), :], qs[rows_at(q_at, COLS), :], 1, 1)
            for q_at, block, _ in todo
        ]
        tops, totals = [], []
        for (_, block, query_pos), score in zip(todo, scores):
            parts = []
            for sub in range(SUBS):
                gap = (query_pos - meta[spans + block * SUBS + sub]) * SPAN
                part = jnp.where(pattern <= gap, score[part_slice(sub, SPAN)] * SCALE2, NEG)
                parts.append(part.reshape(SPAN // 8, 8, COLS))
            top = functools.reduce(jnp.maximum, [jnp.max(part, axis=0) for part in parts])
            tops.append(top)
            totals.append(sum(jnp.sum(jnp.exp2(part - top[None]), axis=0) for part in parts))
        for (q_at, _, _), top, total in zip(todo, tops, totals):
            rows = rows_at(q_at, 8)
            old = ms[rows, :]
            new = jnp.maximum(old, top)
            ls[rows, :] = ls[rows, :] * jnp.exp2(old - new) + total * jnp.exp2(top - new)
            ms[rows, :] = new
    out_ref[2 * QSPANS :, :] = before[2 * QSPANS :, :]
    for i in range(QSPANS):
        run_max, run_sum = ms[part_slice(i, 8), :], ls[part_slice(i, 8), :]
        old_max, old_sum = before[i : i + 1, :], before[QSPANS + i : QSPANS + i + 1, :]
        top = jnp.maximum(jnp.max(run_max, axis=0, keepdims=True), old_max)
        total = jnp.sum(run_sum * jnp.exp2(run_max - top), axis=0, keepdims=True)
        out_ref[i : i + 1, :] = top
        out_ref[QSPANS + i : QSPANS + i + 1, :] = total + old_sum * jnp.exp2(old_max - top)
    for move in moves:
        move.wait()


def grads_kernel(spans, steps, last, *refs):
    meta, k_ref, v_ref = refs[:3]
    blocks, stats, refs = refs[3:7], refs[7:11], refs[11:]
    if last:
        dq_before, dkv_ref, *dq_refs = refs[: 2 + SHARE]
        kin, vin, dkv, own, others, ks, vs, kt, dka, dva, qs, gs, lt, dl, dqa, sems = refs[6:]
    else:
        dkv_ref, dq_ref, kin, vin, dkv, ks, vs, kt, dka, dva, qs, gs, lt, dl, dqa, sems = refs
    copies = load_all(
        (k_ref, v_ref, *[b.at[:, :HEAD] for b in blocks], *[b.at[:, HEAD:] for b in blocks]),
        (
            kin,
            vin,
            *[slot_rows(qs, n) for n in range(SHARE)],
            *[slot_rows(gs, n) for n in range(SHARE)],
        ),
        sems,
    )
    if last:
        before = [dq_before.at[part_slice(n, 2 * HEAD)] for n in range(SHARE)]
        targets = [dqa.at[part_slice(n, 2 * HEAD)] for n in range(SHARE)]
        copies += load_all(before, targets, sems.at[2 * SHARE + 2 :])
    else:
        dqa[...] = jnp.zeros_like(dqa)
    dka[...] = jnp.zeros_like(dka)
    dva[...] = jnp.zeros_like(dva)
    copies[0].wait()
    copies[1].wait()

    def copy_span(n, carry):
        rows = rows_at(n, SPAN)
        ks[rows, :] = kin[rows_at(meta[n], SPAN), :]
        vs[rows, :] = vin[rows_at(meta[n], SPAN), :]
        return carry

    lax.fori_loop(0, spans, copy_span, 0, unroll=8)
    for block in range(spans // SUBS):
        kt[part_slice(block, HEAD), :] = ks[part_slice(block, BLOCK), :].astype(F32).T.astype(BF16)
    pattern = mask_pattern()
    for i in range(QSPANS):
        slot, half = i // 2, i % 2
        delta = stats[slot][2 * QSPANS + half : 2 * QSPANS + half + 1, :]
        dl[part_slice(i, 8), :] = jnp.broadcast_to(delta, (8, COLS))
        tops, sums = [], []
        for shift in range(SHARE):
            row = ((slot - shift) % SHARE) * 2 + half
            tops.append(stats[shift][row : row + 1, :])
            sums.append(stats[shift][QSPANS + row : QSPANS + row + 1, :])
        top = functools.reduce(jnp.maximum, tops)
        total = sum(s * jnp.exp2(t - top) for s, t in zip(sums, tops))
        lt[part_slice(i, 8), :] = jnp.broadcast_to(top + jnp.log(total) * LOG2E, (8, COLS))
    stores = []
    for slot in range(SHARE):
        for copy in copies[2 + slot :: SHARE]:
            copy.wait()
        todo = slot_steps(meta, spans, steps, slot)
        key_rows = [rows_at(block, BLOCK) for _, block, _ in todo]
        query_rows = [rows_at(q_at, COLS) for q_at, _, _ in todo]
        scores, grad_probs = [], []
        for kr, qr in zip(key_rows, query_rows):
            scores.append(dot(ks[kr, :], qs[qr, :], 1, 1))
            grad_probs.append(dot(vs[kr, :], gs[qr, :], 1, 1))
        probs, grad_scores = [], []
        for u, (q_at, block, query_pos) in enumerate(todo):
            log_total, delta = lt[rows_at(q_at, 8), :][None], dl[rows_at(q_at, 8), :][None]
            low, low_grad = [], []
            for sub in range(SUBS):
                gap = (query_pos - meta[spans + block * SUBS + sub]) * SPAN
                rows = part_slice(sub, SPAN)
                part = scores[u][rows].reshape(SPAN // 8, 8, COLS) * SCALE2 - log_total
                part = jnp.where(pattern <= gap, jnp.exp2(part.reshape(SPAN, COLS)), 0.0)
                low.append(part.astype(BF16))
                change = grad_probs[u][rows].reshape(SPAN // 8, 8, COLS) - delta
                low_grad.append((part * change.reshape(SPAN, COLS)).astype(BF16))
            probs.append(jnp.concatenate(low, axis=0))
            grad_scores.append(jnp.concatenate(low_grad, axis=0))
        to_value, to_key, to_query = [], [], []
        for u, (_, block, _) in enumerate(todo):
            to_value.append(dot(probs[u], gs[query_rows[u], :], 1, 0))
            to_key.append(dot(grad_scores[u], qs[query_rows[u], :], 1, 0))
            to_query.append(dot(kt[rows_at(block, HEAD), :], grad_scores[u], 1, 0))
        for u, (q_at, _, _) in enumerate(todo):
            dva[key_rows[u], :] += to_value[u]
            dka[key_rows[u], :] += to_key[u]
            dqa[rows_at(q_at, HEAD), :] += to_query[u]
        store_sem = sems.at[3 * SHARE + 2 + slot]
        if last:
            out = own if slot == 0 else others.at[slot - 1]
            for half in range(2):
                full = dqa[part_slice(2 * slot + half, HEAD), :].T * SCALE
                for h in range(GROUP):
                    out[span_slice(half), head_cols(h)] = full[part_slice(h, SPAN)].astype(out.dtype)
            stores.append(pltpu.make_async_copy(out, dq_refs[slot], store_sem))
        else:
            rows = part_slice(slot, 2 * HEAD)
            stores.append(pltpu.make_async_copy(dqa.at[rows], dq_ref.at[rows], store_sem))
        stores[-1].start()

    def place_span(n, carry):
        rows = rows_at(n, SPAN)
        dest = spans - 2 - meta[n] + 2 * (meta[n] % 2)
        dkv[span_rows(dest, 0), :] = (dka[rows, :] * SCALE).astype(dkv.dtype)
        dkv[span_rows(dest, 1), :] = dva[rows, :].astype(dkv.dtype)
        return carry

    lax.fori_loop(0, spans, place_span, 0, unroll=8)
    stores.append(pltpu.make_async_copy(dkv, dkv_ref, sems.at[4 * SHARE + 2]))
    stores[-1].start()
    for store in stores:
        store.wait()


def project_kernel(
    peers, d0, d1, d2, d3, dkv_ref, narrow_ref, wq_ref, o0, o1, o2, o3,
    own, others, dkv, narrow, sems,
):
    tokens, feats = o0.shape
    copies = load_all(
        (d0, d1, d2, d3, dkv_ref, narrow_ref),
        (own, *[others.at[n] for n in range(SHARE - 1)], dkv, narrow),
        sems,
    )
    for copy in copies[:SHARE]:
        copy.wait()
    query = own[...]
    for n in range(SHARE - 1):
        query = query + others[n].astype(F32)
    query = query.astype(BF16)
    rows = [rows_at(peers[s], feats) for s in range(SHARE)]
    totals = [dot(query, wq_ref[at, :], 1, 1) for at in rows]
    copies[SHARE].wait()
    sums = jnp.zeros((2 * tokens, HEAD), F32)
    for member in range(dkv.shape[0] // (2 * tokens)):
        sums = sums + dkv[part_slice(member, 2 * tokens), :].astype(F32)
    sums = sums.astype(BF16)
    for copy in copies[SHARE + 1 :]:
        copy.wait()
    lower = [rows_at(peers[s] + SHARE, feats) for s in range(SHARE)]
    for at, low, total, out in zip(rows, lower, totals, (o0, o1, o2, o3)):
        total = total + dot(sums[:tokens], narrow[at, :], 1, 1)
        total = total + dot(sums[tokens:], narrow[low, :], 1, 1)
        out[...] = total.astype(out.dtype)


VMEM = pl.BlockSpec(memory_space=pltpu.VMEM)
SMEM = pl.BlockSpec(memory_space=pltpu.SMEM)
HBM = pl.BlockSpec(memory_space=pltpu.HBM)
LARGE = pltpu.CompilerParams(vmem_limit_bytes=60 * 1024 * 1024)
SMALL = pltpu.CompilerParams(vmem_limit_bytes=16 * 1024 * 1024)


def shape(dims, dtype):
    return jax.ShapeDtypeStruct(dims, dtype)


def step_tables(span_pos, side, member, share, members, steps):
    spans = 2 * members
    cut = span_pos.reshape(SIDES, members, SHARE, 2)
    key_pos = lax.dynamic_slice_in_dim(cut, share, 1, axis=2).reshape(SIDES, spans)
    key_pos = jnp.where(side == 0, key_pos, key_pos[::-1])
    ids = jnp.arange(spans, dtype=jnp.int32)
    rank = jnp.sum((key_pos[:, None, :] < key_pos[:, :, None]).astype(jnp.int32), axis=2)
    placed = rank[:, None, :] == ids[None, :, None]
    order = jnp.sum(jnp.where(placed, ids[None, None, :], 0), axis=2)
    sorted_pos = jnp.sum(jnp.where(placed, key_pos[:, None, :], 0), axis=2)
    slots = jnp.arange(SHARE, dtype=jnp.int32)
    source = ((side * members + member) * SHARE + (share + SHARE - slots) % SHARE) * 2
    places = jnp.arange(span_pos.shape[0], dtype=jnp.int32)
    query_pos = [
        jnp.sum(jnp.where(places[None, :] == source[:, None] + h, span_pos[None, :], 0), axis=1)
        for h in range(2)
    ]
    blocks = [
        (jnp.sum((key_pos[:, None, :] <= qp[None, :, None]).astype(jnp.int32), axis=2) + SUBS - 1)
        // SUBS
        for qp in query_pos
    ]
    first, other = blocks[0][:, :, None], blocks[1][:, :, None]
    at = jnp.arange(steps // SHARE, dtype=jnp.int32)[None, None, :]
    second = at >= first
    block = jnp.where(second, at - first, at)
    used = jnp.logical_or(jnp.logical_not(second), block < other)
    q_at = jnp.where(second, 1, 0) + 2 * slots[None, :, None]
    pos = jnp.where(second, query_pos[1][None, :, None], query_pos[0][None, :, None])
    table = jnp.stack([q_at, jnp.where(used, block, 0), jnp.where(used, pos, -1)], axis=3)
    return jnp.concatenate([order, sorted_pos, table.reshape(SIDES, -1)], axis=1)


def local(q, k, v, o, g, w_query, key_weight, value_weight, span_pos):
    tokens = q.shape[0]
    cycle = lax.axis_size("ctx")
    tp_size = lax.axis_size("tp")
    members = cycle // SHARE // SIDES
    spans = 2 * members
    half_rows = 2 * spans * SPAN
    steps = SHARE * ((spans + 1 + 2 * (SUBS - 1)) // SUBS)
    index = lax.axis_index("ctx")
    share, member, side = index % SHARE, index // SHARE % members, index // (SHARE * members)

    def device(side_at, member_at, share_at):
        return (side_at % SIDES * members + member_at) * SHARE + share_at % SHARE

    places = [(a, b, c) for a in range(SIDES) for b in range(members) for c in range(SHARE)]
    key_groups = [
        [device(a, b, c) for b in range(members)] for a in range(SIDES) for c in range(SHARE)
    ]

    def exchanged(array, groups):
        return lax.all_to_all(array, "ctx", 0, 0, tiled=True, axis_index_groups=groups)

    def shifted(array, by):
        return lax.ppermute(array, "ctx", [(device(a, b, c), device(a, b, c + by)) for a, b, c in places])

    def crossed(array):
        return lax.ppermute(array, "ctx", [(device(a, b, c), device(a + 1, b, c)) for a, b, c in places])

    copies, block, start = pl.pallas_call(
        pack_kernel,
        out_shape=[
            shape((half_rows, HEAD), BF16),
            shape((2 * COLS, 2 * HEAD), BF16),
            shape((STATS, COLS), F32),
        ],
        in_specs=[VMEM] * 5,
        out_specs=[VMEM] * 3,
        name="pack",
    )(k, v, q, g, o)
    kv_own = exchanged(copies, key_groups)
    blocks = [block] + [shifted(block, s) for s in range(1, SHARE)]
    meta = step_tables(span_pos, side, member, share, members, steps)
    meta_own, meta_other = meta[0], meta[1]
    sides = kv_own.reshape(members, 2, tokens, HEAD)
    k_own, v_own = [sides[:, n].reshape(spans * SPAN, HEAD) for n in range(2)]
    k_other = crossed(k_own)

    def stats_of(table, keys, before, weights):
        return pl.pallas_call(
            functools.partial(stats_kernel, spans, steps),
            out_shape=[shape((STATS, COLS), F32)]
            + [shape((2 * w.shape[0], HEAD), BF16) for w in weights[:1]],
            in_specs=[SMEM] + [HBM] * 5 + [VMEM] + [HBM] * len(weights),
            out_specs=[VMEM] + [HBM] * len(weights[:1]),
            scratch_shapes=[
                *[pltpu.VMEM((2 * w.shape[0], HEAD), BF16) for w in weights[:1]],
                pltpu.VMEM((spans * SPAN, HEAD), BF16),
                pltpu.VMEM((spans * SPAN, HEAD), BF16),
                pltpu.VMEM((QSPANS * COLS, HEAD), BF16),
                pltpu.VMEM((QSPANS * 8, COLS), F32),
                pltpu.VMEM((QSPANS * 8, COLS), F32),
                pltpu.SemaphoreType.DMA((8,)),
            ],
            compiler_params=SMALL,
            cost_estimate=pl.CostEstimate(
                flops=1 << 30, bytes_accessed=1 << 22, transcendentals=1 << 22
            ),
            name="stats",
        )(table, keys, *blocks, before, *weights)

    stats_own, narrow = stats_of(meta_own, k_own, start, [key_weight, value_weight])
    stats_own, v_late = lax.optimization_barrier((stats_own, v_own))
    v_other = crossed(v_late)
    (stats,) = stats_of(meta_other, k_other, stats_own, [])
    all_stats = [stats] + [shifted(stats, s) for s in range(1, SHARE)]

    def grads_of(table, keys, values, last, extra_in, outs, extra_scratch):
        return pl.pallas_call(
            functools.partial(grads_kernel, spans, steps, last),
            out_shape=outs,
            in_specs=[SMEM] + [HBM] * 6 + [VMEM] * 4 + [HBM] * len(extra_in),
            out_specs=[HBM] * len(outs),
            scratch_shapes=[
                pltpu.VMEM((spans * SPAN, HEAD), BF16),
                pltpu.VMEM((spans * SPAN, HEAD), BF16),
                pltpu.VMEM((half_rows, HEAD), outs[0].dtype),
                *extra_scratch,
                pltpu.VMEM((spans * SPAN, HEAD), BF16),
                pltpu.VMEM((spans * SPAN, HEAD), BF16),
                pltpu.VMEM((spans // SUBS * HEAD, BLOCK), BF16),
                pltpu.VMEM((spans * SPAN, HEAD), F32),
                pltpu.VMEM((spans * SPAN, HEAD), F32),
                pltpu.VMEM((QSPANS * COLS, HEAD), BF16),
                pltpu.VMEM((QSPANS * COLS, HEAD), BF16),
                pltpu.VMEM((QSPANS * 8, COLS), F32),
                pltpu.VMEM((QSPANS * 8, COLS), F32),
                pltpu.VMEM((QSPANS * HEAD, COLS), F32),
                pltpu.SemaphoreType.DMA((4 * SHARE + 3,)),
            ],
            compiler_params=LARGE,
            cost_estimate=pl.CostEstimate(
                flops=1 << 31, bytes_accessed=1 << 23, transcendentals=1 << 22
            ),
            name="grads",
        )(table, keys, values, *blocks, *all_stats, *extra_in)

    dkv_other, dq_before = grads_of(
        meta_other,
        k_other,
        v_other,
        False,
        [],
        [shape((half_rows, HEAD), BF16), shape((QSPANS * HEAD, COLS), F32)],
        [],
    )
    dkv_crossed = crossed(dkv_other)
    dkv_own, *dqs = grads_of(
        meta_own,
        k_own,
        v_own,
        True,
        [dq_before],
        [shape((half_rows, HEAD), BF16), shape((tokens, WIDTH), F32)]
        + [shape((tokens, WIDTH), BF16)] * (SHARE - 1),
        [pltpu.VMEM((tokens, WIDTH), F32), pltpu.VMEM((SHARE - 1, tokens, WIDTH), BF16)],
    )
    turned_groups = [group[::-1] for group in key_groups]
    dkv_parts = exchanged((dkv_own.astype(F32) + dkv_crossed.astype(F32)).astype(BF16), turned_groups)
    dq_parts = [shifted(dqs[s], -s) for s in range(1, SHARE)]
    peers = (lax.axis_index("tp") + jnp.arange(tp_size, dtype=jnp.int32)) % tp_size
    feats = w_query.shape[0] // tp_size
    own, *pieces = pl.pallas_call(
        project_kernel,
        out_shape=[shape((tokens, feats), F32)] + [shape((tokens, feats), BF16)] * (tp_size - 1),
        in_specs=[SMEM] + [HBM] * 6 + [VMEM],
        out_specs=[VMEM] * tp_size,
        scratch_shapes=[
            pltpu.VMEM((tokens, WIDTH), F32),
            pltpu.VMEM((SHARE - 1, tokens, WIDTH), BF16),
            pltpu.VMEM((half_rows, HEAD), BF16),
            pltpu.VMEM(narrow.shape, BF16),
            pltpu.SemaphoreType.DMA((6,)),
        ],
        compiler_params=SMALL,
        name="project",
    )(peers, dqs[0], *dq_parts, dkv_parts, narrow, w_query)
    for s in range(1, tp_size):
        pairs = [(d, (d + s) % tp_size) for d in range(tp_size)]
        own = own + lax.ppermute(pieces[s - 1], "tp", pairs).astype(F32)
    return own.astype(BF16)


def solution(mesh):
    row, col = P("ctx", "tp"), P(None, "tp")
    in_specs = (row, row, row, row, row, col, col, col, P())
    return jax.shard_map(local, mesh=mesh, in_specs=in_specs, out_specs=row, check_vma=False)
```
